32 devices in a mesh: pipe: 4 (over z), expert: 8 (over y, x, core).
Axes of the slice: x: 2, y: 2, z: 4, core: 2. Of those that a mesh axis runs over, the one named last changes fastest.
Arguments:
- forward_input: bfloat16 [4, 1024, 2048], P('pipe', 'expert'), may hold values from -6 to 6
- queries: bfloat16 [4, 1024, 2048], P('pipe', 'expert'), may hold values from -100 to 100
- new_keys: bfloat16 [4, 1024, 256], P('pipe', 'expert'), may hold values from -6 to 6
- new_values: bfloat16 [4, 1024, 256], P('pipe', 'expert'), may hold values from -6 to 6
- cache_keys: bfloat16 [4, 1024, 256], P('pipe', 'expert'), may hold values from -6 to 6
- cache_values: bfloat16 [4, 1024, 256], P('pipe', 'expert'), may hold values from -6 to 6
- context_lengths: int32 [4, 8], P('pipe', 'expert'), may hold values from 1 to 128
- norm_gain: float32 [4, 2048], P('pipe'), may hold values from 0.5 to 1.5
- router: bfloat16 [4, 2048, 8], P('pipe'), may hold values from -0.125 to 0.125
- gate_weight: bfloat16 [4, 8, 2048, 768], P('pipe', 'expert'), may hold values from -0.125 to 0.125
- up_weight: bfloat16 [4, 8, 2048, 768], P('pipe', 'expert'), may hold values from -0.125 to 0.125
- down_weight: bfloat16 [4, 8, 768, 2048], P('pipe', 'expert'), may hold values from -0.21875 to 0.21875
- forward_ids: int32 [4, 1024, 4], P('pipe', 'expert'), may hold values from 0 to 7, all different within a row; in each aligned block of 128 rows (0 to 127, 128 to 255, ..., all dimensions but the last counted through in order) at most 72 rows name the same one
- backward_input: bfloat16 [4, 1024, 2048], P('pipe', 'expert'), may hold values from -6 to 6
- backward_ids: int32 [4, 1024, 4], P('pipe', 'expert'), may hold values from 0 to 7, all different within a row; in each aligned block of 128 rows (0 to 127, 128 to 255, ..., all dimensions but the last counted through in order) at most 72 rows name the same one
- output_grad: bfloat16 [4, 1024, 2048], P('pipe', 'expert'), may hold values from -6 to 6
Outputs:
- forward_output: bfloat16 [4, 1024, 2048], P('pipe', 'expert')
- input_grad: bfloat16 [4, 1024, 2048], P('pipe', 'expert')
- router_grad: float32 [4, 2048, 8], P('pipe', 'expert')
- gain_grad: float32 [4, 2048], P('pipe', 'expert')
The draws below stay inside these ranges and needn't reach their ends.
Inputs may be any that keep to these rules, and one draw needn't show every extreme that they name: `forward_ids`: each row names 4 different experts; in the 128 rows of one device no expert is named more than 72 times, and on some devices one is named exactly 72 times. `backward_ids`: each row names 4 different experts; in the 128 rows of one device no expert is named more than 72 times, and on some devices one is named exactly 72 times.
All inputs are finite; a program needn't handle non-finite values.
Results may differ from the reference program's by a relative error of at most 0.012.
Values may be sent and summed in bfloat16 or wider, within the bound.
A program may use at most 128 MiB of HBM per device.

```python
import math
import jax
import jax.numpy as jnp
import numpy as np
from jax import lax

D = 2048
FF = 768
HEADS = 16
KV_HEADS = 2
HEAD_DIM = 128
TOP = 4
CTX = 128
TOK_DEV = 128
EXPERTS = 8
MOST = 72
TOKENS = 1024
SEQS = 8
N_PIPE = 4
N_EXPERT = 8


def plant_pair(key):
    base = jax.random.fold_in(key, 31)
    key_query, key_keys = jax.random.split(base, 2)
    keys_all = jnp.clip(jax.random.normal(key_keys, (N_PIPE, TOKENS, KV_HEADS, HEAD_DIM), jnp.float32), -5.0, 5.0)
    query_all = jnp.clip(jax.random.normal(key_query, (N_PIPE, TOKENS, HEADS, HEAD_DIM), jnp.float32), -5.0, 5.0)
    return (query_all.reshape(N_PIPE, TOKENS, HEADS * HEAD_DIM), keys_all.reshape(N_PIPE, TOKENS, KV_HEADS * HEAD_DIM))


def draw_queries(key, part):
    return plant_pair(key)[0].astype(jnp.bfloat16)


def draw_new_keys(key, part):
    return plant_pair(key)[1].astype(jnp.bfloat16)


def touch_ends(array, rng, least, largest):
    dims = array.shape
    index_at = [jax.random.randint(jax.random.fold_in(rng, axis), (), 0, dims[axis]) for axis in range(len(dims))]
    array = array.at[tuple(index_at)].set(least)
    longest = dims.index(max(dims))
    index_at[longest] = (index_at[longest] + 1) % dims[longest]
    return array.at[tuple(index_at)].set(largest)


def strengthened(drawn, own_key, source, target, blocks, factor):
    def block_of(dim):
        return (jnp.arange(drawn.shape[dim]) // (drawn.shape[dim] // blocks)).reshape((-1,) + (1,) * (drawn.ndim - 1 - dim))

    one_side = jax.random.permutation(own_key, blocks)[block_of(target)]
    other_side = (block_of(target) + blocks // 2) % blocks
    return jnp.where((block_of(source) == one_side) | (block_of(source) == other_side), factor * drawn, drawn)


def shard_levels(rng, dims, shards, least, high):
    loudness = 1.0
    for dim, parts in shards:
        draws = jax.random.uniform(jax.random.fold_in(jax.random.fold_in(rng, 6), dim), (parts,), jnp.float32, least / len(shards), high / len(shards))
        loudness = loudness * jnp.repeat(jnp.exp(draws), dims[dim] // parts).reshape((-1,) + (1,) * (len(dims) - 1 - dim))
    return loudness


def deal_out(rng, own, number, rows, count, top, bound, slope):
    sequence = jax.random.permutation(rng, count)
    heavy_load, usual = portions_of(count, rows * top, bound, slope, True), portions_of(count, rows * top, bound, slope, False)
    places = jnp.arange(count)

    def named(tallies, rotation):
        used = int((tallies > 0).sum())
        fixed = max(1, used // 4)
        moved = fixed + (places - fixed + rotation * (used - fixed)) % max(1, count - fixed)
        return jnp.zeros((count,), jnp.int32).at[sequence[jnp.where(places < fixed, places, moved)]].set(jnp.asarray(tallies, jnp.int32))

    tallies = jnp.where(number % 4 == 0, named(heavy_load, number // 4), named(usual, number - number // 4 - 1))
    mixed = jax.random.permutation(jax.random.fold_in(own, 3), count)
    donor, receiver = mixed[0:count // 2 * 2:2], mixed[1:count // 2 * 2:2]
    room = jnp.minimum(tallies[donor] - 1, bound - tallies[receiver]) // 2
    room = jnp.where((donor == sequence[0]) | (receiver == sequence[0]) | (tallies[receiver] == 0), 0, jnp.maximum(room, 0))
    moved = jax.random.randint(jax.random.fold_in(own, 4), (count // 2,), 0, 1 << 20) % (room + 1)
    tallies = tallies.at[donor].add(-moved).at[receiver].add(moved)
    labels = jnp.searchsorted(jnp.cumsum(tallies), jnp.arange(rows * top), side="right").astype(jnp.int32)
    grid = labels.reshape(top, rows).T
    grid = grid[jax.random.permutation(jax.random.fold_in(own, 1), rows)]
    rotation = jax.random.randint(jax.random.fold_in(own, 2), (rows, 1), 0, top)
    return jnp.take_along_axis(grid, (jnp.arange(top)[None, :] + rotation) % top, axis=1)


def portions_of(amount, total, reach, slope, full):
    loads = [(1 << 20) // math.isqrt(standing ** slope) + 1 for standing in range(1, amount + 1)]
    largest = reach if full else min(reach, max(-(-total // amount), total * loads[0] // sum(loads)))
    least = 1 if total - largest >= amount - 1 else 0
    given, spare = [largest] + [least] * (amount - 1), total - largest - least * (amount - 1)
    while spare > 0:
        movable = [i for i in range(1, amount) if given[i] < largest] or [i for i in range(1, amount) if given[i] < reach]
        whole, left = sum([loads[i] for i in movable]), spare
        for i in movable:
            addition = min(reach - given[i], max(1, left * loads[i] // whole), spare)
            given[i] = given[i] + addition
            spare = spare - addition
    return np.array(given)


def normal_values(key, extent, deviation, limit, cuts=(), kind=jnp.bfloat16):
    loudness = shard_levels(key, extent, cuts, -0.22, 0.18) if cuts else 1.0
    drawn = jax.random.normal(key, extent, jnp.float32) * deviation * loudness
    return jnp.minimum(jnp.maximum(drawn, -limit), limit).astype(kind)


def gaussian_with(key, dims, width, limit, pieces, heavy, kind=jnp.bfloat16):
    drawn = width * jax.random.normal(key, dims, jnp.float32)
    if pieces:
        drawn = drawn * shard_levels(key, dims, pieces, -0.22, 0.18)
    return jnp.clip(strengthened(drawn, jax.random.fold_in(key, 3), *heavy), -limit, limit).astype(kind)


def setup_inputs(seed: int = 0) -> dict:
    keys = jax.random.split(jax.random.key(seed), 17)
    forward_input = normal_values(keys[0], (N_PIPE, TOKENS, D), 1.0, 6.0, ((0, 4), (1, 8)))
    queries = draw_queries(jax.random.fold_in(keys[16], 71), 0)
    new_keys = draw_new_keys(jax.random.fold_in(keys[16], 71), 0)
    new_values = normal_values(keys[3], (N_PIPE, TOKENS, KV_HEADS * HEAD_DIM), 1.0, 6.0, ((0, 4), (1, 8)))
    cache_keys = normal_values(keys[4], (N_PIPE, SEQS * CTX, KV_HEADS * HEAD_DIM), 1.0, 6.0, ((0, 4), (1, 8)))
    cache_values = normal_values(keys[5], (N_PIPE, SEQS * CTX, KV_HEADS * HEAD_DIM), 1.0, 6.0, ((0, 4), (1, 8)))
    context_lengths = touch_ends(jax.random.randint(keys[6], (N_PIPE, SEQS), 1, CTX + 1), jax.random.fold_in(keys[6], 1), 1, CTX).astype(jnp.int32)
    norm_gain = jnp.clip(1.0 + 0.1 * jax.random.normal(keys[7], (N_PIPE, D), jnp.float32), 0.5, 1.5)
    router = normal_values(keys[8], (N_PIPE, D, EXPERTS), D ** -0.5, 0.125, ((0, 4),))
    gate_weight = normal_values(keys[9], (N_PIPE, EXPERTS, D, FF), D ** -0.5, 0.125, ((0, 4), (1, 8)))
    up_weight = normal_values(keys[10], (N_PIPE, EXPERTS, D, FF), D ** -0.5, 0.125, ((0, 4), (1, 8)))
    down_weight = normal_values(keys[11], (N_PIPE, EXPERTS, FF, D), FF ** -0.5, 0.21875, ((0, 4), (1, 8)))
    forward_ids_keys = jax.random.split(jax.random.fold_in(keys[12], 1), N_PIPE * TOKENS // TOK_DEV)
    forward_ids_turns = jax.random.permutation(jax.random.fold_in(keys[12], 3), N_PIPE * TOKENS // TOK_DEV)
    forward_ids = jax.vmap(lambda own, number: deal_out(jax.random.fold_in(keys[12], 2), own, number, TOK_DEV, EXPERTS, TOP, MOST, 2))(forward_ids_keys, forward_ids_turns).reshape((N_PIPE, TOKENS, TOP))
    backward_input = normal_values(keys[13], (N_PIPE, TOKENS, D), 1.0, 6.0, ((0, 4), (1, 8)))
    backward_ids_keys = jax.random.split(jax.random.fold_in(keys[14], 1), N_PIPE * TOKENS // TOK_DEV)
    backward_ids_turns = jax.random.permutation(jax.random.fold_in(keys[14], 3), N_PIPE * TOKENS // TOK_DEV)
    backward_ids = jax.vmap(lambda own, number: deal_out(jax.random.fold_in(keys[14], 2), own, number, TOK_DEV, EXPERTS, TOP, MOST, 2))(backward_ids_keys, backward_ids_turns).reshape((N_PIPE, TOKENS, TOP))
    output_grad = gaussian_with(keys[15], (N_PIPE, TOKENS, D), 1.0, 6.0, ((0, 4), (1, 8)), (1, 2, 8, 2.0))
    return dict(forward_input=forward_input, queries=queries, new_keys=new_keys, new_values=new_values, cache_keys=cache_keys, cache_values=cache_values, context_lengths=context_lengths, norm_gain=norm_gain, router=router, gate_weight=gate_weight, up_weight=up_weight, down_weight=down_weight, forward_ids=forward_ids, backward_input=backward_input, backward_ids=backward_ids, output_grad=output_grad)


epsilon = 1e-06
far_below = -1e+30

def normalize(resid, gain):
    wide = resid.astype(jnp.float32)
    inv_rms = lax.rsqrt(lax.optimization_barrier(jnp.mean(wide * wide, axis=-1, keepdims=True)) + epsilon)
    return (wide, inv_rms, (wide * inv_rms * gain).astype(jnp.bfloat16))

def routing(normed, expert_ids, table):
    logits = jnp.dot(normed.astype(jnp.float32), table.astype(jnp.float32))
    selects = expert_ids[:, :, None] == jnp.arange(table.shape[1], dtype=jnp.int32)
    chosen = lax.optimization_barrier(jnp.sum(jnp.where(selects, logits[:, None, :], 0.0), axis=-1))
    route_probs = 1.0 / lax.optimization_barrier(jnp.sum(jnp.exp(chosen[:, None, :] - chosen[:, :, None]), axis=-1))
    return (route_probs, selects)

def place_slots(selects, capacity):
    counted = selects.reshape(-1, selects.shape[-1]).astype(jnp.int32)
    running = jnp.cumsum(counted, axis=0)
    slot_index = lax.optimization_barrier(jnp.sum(counted * running, axis=-1)) - 1
    owner = lax.optimization_barrier(jnp.sum(counted * jnp.arange(selects.shape[-1], dtype=jnp.int32), axis=-1))
    return (owner * capacity + slot_index).reshape(selects.shape[0], selects.shape[1])

def attention(queries, new_keys, new_values, cache_keys, cache_values, length):
    tokens = queries.shape[0]
    context = cache_keys.shape[0]
    key_rows = jnp.concatenate([cache_keys, new_keys], axis=0).astype(jnp.float32).reshape(-1, KV_HEADS, HEAD_DIM)
    value_rows = jnp.concatenate([cache_values, new_values], axis=0).astype(jnp.float32).reshape(-1, KV_HEADS, HEAD_DIM)
    grouped = queries.astype(jnp.float32).reshape(tokens, KV_HEADS, HEADS // KV_HEADS, HEAD_DIM)
    scores = jnp.einsum('tkgd,skd->kgts', grouped, key_rows) * HEAD_DIM ** (-0.5)
    position = jnp.arange(key_rows.shape[0], dtype=jnp.int32)[None, :]
    query_pos = jnp.arange(tokens, dtype=jnp.int32)[:, None]
    visible = jnp.where(position < context, position < length, position - context <= query_pos)
    scores = jnp.where(visible, scores, far_below)
    row_max = lax.optimization_barrier(jnp.max(scores, axis=-1, keepdims=True))
    lifted = jnp.exp(scores - row_max)
    attn_weights = (lifted / lax.optimization_barrier(jnp.sum(lifted, axis=-1, keepdims=True))).astype(jnp.bfloat16)
    merged = jnp.einsum('kgts,skd->tkgd', attn_weights.astype(jnp.float32), value_rows)
    return merged.reshape(tokens, HEADS * HEAD_DIM).astype(jnp.bfloat16)

def expert_ahead(operands):
    slot_rows, gate_matrix, up_matrix, down_matrix = operands
    wide_rows = slot_rows.astype(jnp.float32)
    gate_pre = jnp.dot(wide_rows, gate_matrix.astype(jnp.float32))
    up_pre = jnp.dot(wide_rows, up_matrix.astype(jnp.float32))
    hidden = (gate_pre * jax.nn.sigmoid(gate_pre) * up_pre).astype(jnp.bfloat16)
    return jnp.dot(hidden.astype(jnp.float32), down_matrix.astype(jnp.float32)).astype(jnp.bfloat16)

def expert_behind(operands):
    slot_rows, slot_grads, gate_matrix, up_matrix, down_matrix = operands
    wide_rows = slot_rows.astype(jnp.float32)
    gate_wide = gate_matrix.astype(jnp.float32)
    up_wide = up_matrix.astype(jnp.float32)
    gate_pre = jnp.dot(wide_rows, gate_wide)
    up_pre = jnp.dot(wide_rows, up_wide)
    sigmoid_gate = jax.nn.sigmoid(gate_pre)
    gate_act = gate_pre * sigmoid_gate
    hidden = (gate_act * up_pre).astype(jnp.bfloat16)
    down_grad = jnp.dot(slot_grads.astype(jnp.float32), down_matrix.astype(jnp.float32).T)
    weight_grad = lax.optimization_barrier(jnp.sum(hidden.astype(jnp.float32) * down_grad, axis=-1)).astype(jnp.bfloat16)
    slope_act = sigmoid_gate * (1.0 + gate_pre * (1.0 - sigmoid_gate))
    gate_grad = (down_grad * up_pre * slope_act).astype(jnp.bfloat16)
    up_grad = (down_grad * gate_act).astype(jnp.bfloat16)
    slot_back = jnp.dot(gate_grad.astype(jnp.float32), gate_wide.T) + jnp.dot(up_grad.astype(jnp.float32), up_wide.T)
    return (slot_back.astype(jnp.bfloat16), weight_grad)

def layout(selects):
    target = jax.vmap(lambda picked: place_slots(picked, MOST))(selects.reshape(N_EXPERT, TOK_DEV, TOP, EXPERTS))
    owner = target // MOST
    column = jnp.arange(N_EXPERT, dtype=jnp.int32)[:, None, None] * MOST + target % MOST
    return (owner.reshape(TOKENS, TOP), column.reshape(TOKENS, TOP))

def pack_rows(source_rows, owner, column):
    buffer = jnp.zeros((EXPERTS, N_EXPERT * MOST, D), jnp.bfloat16)
    spread = jnp.broadcast_to(source_rows[:, None, :], (TOKENS, TOP, D))
    return buffer.at[owner, column].set(spread)

def section_pass(forward_input, queries, new_keys, new_values, cache_keys, cache_values, context_lengths, norm_gain, router, gate_weight, up_weight, down_weight, forward_ids, backward_input, backward_ids, output_grad):
    sequences = lax.map(lambda operands: attention(*operands), (queries.reshape(N_EXPERT, TOK_DEV, -1), new_keys.reshape(N_EXPERT, TOK_DEV, -1), new_values.reshape(N_EXPERT, TOK_DEV, -1), cache_keys.reshape(N_EXPERT, CTX, -1), cache_values.reshape(N_EXPERT, CTX, -1), context_lengths))
    mixed = sequences.reshape(TOKENS, D)
    resid_ahead = (forward_input.astype(jnp.float32) + mixed.astype(jnp.float32)).astype(jnp.bfloat16)
    ahead_wide, ahead_inv, ahead_normed = normalize(resid_ahead, norm_gain)
    ahead_probs, ahead_selects = routing(ahead_normed, forward_ids, router)
    ahead_owner, ahead_column = layout(ahead_selects)
    ahead_buffer = pack_rows(ahead_normed, ahead_owner, ahead_column)
    produced = lax.map(expert_ahead, (ahead_buffer, gate_weight, up_weight, down_weight))
    ahead_rows = produced[ahead_owner, ahead_column].astype(jnp.float32)
    forward_output = (ahead_wide + lax.optimization_barrier(jnp.sum(ahead_probs[:, :, None] * ahead_rows, axis=1))).astype(jnp.bfloat16)
    behind_wide, behind_inv, behind_normed = normalize(backward_input, norm_gain)
    behind_probs, behind_selects = routing(behind_normed, backward_ids, router)
    behind_owner, behind_column = layout(behind_selects)
    rows_buffer = pack_rows(behind_normed, behind_owner, behind_column)
    grads_buffer = pack_rows(output_grad, behind_owner, behind_column)
    slot_back, slot_weight = lax.map(expert_behind, (rows_buffer, grads_buffer, gate_weight, up_weight, down_weight))
    input_rows = slot_back[behind_owner, behind_column].astype(jnp.float32)
    weight_rows = slot_weight[behind_owner, behind_column].astype(jnp.float32)
    normed_grad = lax.optimization_barrier(jnp.sum(behind_probs[:, :, None] * input_rows, axis=1))
    logit_terms = behind_probs * (weight_rows - lax.optimization_barrier(jnp.sum(behind_probs * weight_rows, axis=-1, keepdims=True)))
    logit_grad = lax.optimization_barrier(jnp.sum(jnp.where(behind_selects, logit_terms[:, :, None], 0.0), axis=1)).astype(jnp.bfloat16)
    normed_grad = normed_grad + jnp.dot(logit_grad.astype(jnp.float32), router.astype(jnp.float32).T)
    grad_factor = TOKENS ** (-0.5)
    router_grad = jnp.dot(behind_normed.astype(jnp.float32).T, logit_grad.astype(jnp.float32)) * grad_factor
    scaled_grad = normed_grad * norm_gain
    resid_grad = behind_inv * (scaled_grad - behind_wide * behind_inv * behind_inv * lax.optimization_barrier(jnp.mean(scaled_grad * behind_wide, axis=-1, keepdims=True)))
    gain_grad = lax.optimization_barrier(jnp.sum(normed_grad * behind_wide * behind_inv, axis=0)) * grad_factor
    input_grad = (output_grad.astype(jnp.float32) + resid_grad).astype(jnp.bfloat16)
    return (forward_output, input_grad, router_grad, gain_grad)

def reference(forward_input, queries, new_keys, new_values, cache_keys, cache_values, context_lengths, norm_gain, router, gate_weight, up_weight, down_weight, forward_ids, backward_input, backward_ids, output_grad):
    outputs = []
    for section in range(N_PIPE):
        outputs.append(section_pass(forward_input[section], queries[section], new_keys[section], new_values[section], cache_keys[section], cache_values[section], context_lengths[section], norm_gain[section], router[section], gate_weight[section], up_weight[section], down_weight[section], forward_ids[section], backward_input[section], backward_ids[section], output_grad[section]))
    forward_output = jnp.roll(jnp.stack([item[0] for item in outputs]), 1, axis=0)
    input_grad = jnp.roll(jnp.stack([item[1] for item in outputs]), -1, axis=0)
    router_grad = jnp.stack([item[2] for item in outputs])
    gain_grad = jnp.stack([item[3] for item in outputs])
    return (forward_output, input_grad, router_grad, gain_grad)
```

```python
import jax
import jax.numpy as jnp
from jax import lax
from jax.sharding import PartitionSpec as P

HEADS = 16
KV_HEADS = 2
HEAD_DIM = 128


epsilon = 1e-06
far_below = -1e30


def extended(x, sides, width):
    for axis, dim in sides:
        devices, length = (lax.axis_size(axis), x.shape[dim])
        up = [(i, (i + 1) % devices) for i in range(devices)]
        down = [(j, i) for i, j in up]
        last = lax.slice_in_dim(x, length - width, length, axis=dim)
        leading = lax.slice_in_dim(x, 0, width, axis=dim)
        before = lax.ppermute(last, axis, up)
        after = lax.ppermute(leading, axis, down)
        x = jnp.concatenate([before, x, after], axis=dim)
    return x


def normalize(resid, gain):
    wide = resid.astype(jnp.float32)
    inv_rms = lax.rsqrt(jnp.mean(wide * wide, axis=-1, keepdims=True) + epsilon)
    return (wide, inv_rms, (wide * inv_rms * gain).astype(jnp.bfloat16))


def routing(normed, expert_ids, table):
    logits = jnp.dot(normed, table, preferred_element_type=jnp.float32)
    selects = expert_ids[:, :, None] == jnp.arange(table.shape[1], dtype=jnp.int32)
    chosen = jnp.sum(jnp.where(selects, logits[:, None, :], 0.0), axis=-1)
    route_probs = 1.0 / jnp.sum(jnp.exp(chosen[:, None, :] - chosen[:, :, None]), axis=-1)
    return (route_probs, selects)


def place_slots(selects, capacity):
    counted = selects.reshape(-1, selects.shape[-1]).astype(jnp.int32)
    running = jnp.cumsum(counted, axis=0)
    slot_index = jnp.sum(counted * running, axis=-1) - 1
    owner = jnp.sum(counted * jnp.arange(selects.shape[-1], dtype=jnp.int32), axis=-1)
    return (owner * capacity + slot_index).reshape(selects.shape[0], selects.shape[1])


def pack_rows(source_rows, target, experts, capacity):
    buffer = jnp.zeros((experts * capacity, source_rows.shape[1]), source_rows.dtype)
    spread = jnp.broadcast_to(source_rows[:, None, :], target.shape + (source_rows.shape[1],))
    return buffer.at[target].set(spread).reshape(experts, capacity, source_rows.shape[1])


def unpack_rows(buffer, target):
    return buffer.reshape((-1,) + buffer.shape[2:])[target]


def gather_slots(received, per_device):
    shaped = received.reshape((-1, per_device) + received.shape[1:])
    return jnp.swapaxes(shaped, 0, 1).reshape((per_device, -1) + received.shape[2:])


def scatter_slots(result, sources):
    shaped = result.reshape((result.shape[0], sources, -1) + result.shape[2:])
    return jnp.swapaxes(shaped, 0, 1).reshape((-1,) + shaped.shape[2:])


def attention(queries, new_keys, new_values, cache_keys, cache_values, length):
    tokens = queries.shape[0]
    context = cache_keys.shape[0]
    key_rows = jnp.concatenate([cache_keys, new_keys], axis=0).reshape(-1, KV_HEADS, HEAD_DIM)
    value_rows = jnp.concatenate([cache_values, new_values], axis=0).reshape(-1, KV_HEADS, HEAD_DIM)
    grouped = queries.reshape(tokens, KV_HEADS, HEADS // KV_HEADS, HEAD_DIM)
    scores = jnp.einsum(
        "tkgd,skd->kgts", grouped, key_rows, preferred_element_type=jnp.float32
    ) * HEAD_DIM ** (-0.5)
    position = jnp.arange(key_rows.shape[0], dtype=jnp.int32)[None, :]
    query_pos = jnp.arange(tokens, dtype=jnp.int32)[:, None]
    visible = jnp.where(position < context, position < length, position - context <= query_pos)
    scores = jnp.where(visible, scores, far_below)
    row_max = jnp.max(scores, axis=-1, keepdims=True)
    lifted = jnp.exp(scores - row_max)
    attn_weights = (lifted / jnp.sum(lifted, axis=-1, keepdims=True)).astype(jnp.bfloat16)
    merged = jnp.einsum(
        "kgts,skd->tkgd", attn_weights, value_rows, preferred_element_type=jnp.float32
    )
    return merged.reshape(tokens, HEADS * HEAD_DIM).astype(jnp.bfloat16)


def expert_ahead(slot_rows, gate_matrix, up_matrix, down_matrix):
    gate_pre = jnp.einsum(
        "erd,edf->erf", slot_rows, gate_matrix, preferred_element_type=jnp.float32
    )
    up_pre = jnp.einsum("erd,edf->erf", slot_rows, up_matrix, preferred_element_type=jnp.float32)
    hidden = (gate_pre * jax.nn.sigmoid(gate_pre) * up_pre).astype(jnp.bfloat16)
    return jnp.einsum(
        "erf,efd->erd", hidden, down_matrix, preferred_element_type=jnp.float32
    ).astype(jnp.bfloat16)


def expert_behind(slot_rows, slot_grads, gate_matrix, up_matrix, down_matrix):
    gate_pre = jnp.einsum(
        "erd,edf->erf", slot_rows, gate_matrix, preferred_element_type=jnp.float32
    )
    up_pre = jnp.einsum("erd,edf->erf", slot_rows, up_matrix, preferred_element_type=jnp.float32)
    sigmoid_gate = jax.nn.sigmoid(gate_pre)
    gate_act = gate_pre * sigmoid_gate
    hidden = (gate_act * up_pre).astype(jnp.bfloat16)
    down_grad = jnp.einsum(
        "erd,efd->erf", slot_grads, down_matrix, preferred_element_type=jnp.float32
    )
    weight_grad = jnp.sum(hidden.astype(jnp.float32) * down_grad, axis=-1).astype(jnp.bfloat16)
    slope_act = sigmoid_gate * (1.0 + gate_pre * (1.0 - sigmoid_gate))
    gate_grad = (down_grad * up_pre * slope_act).astype(jnp.bfloat16)
    up_grad = (down_grad * gate_act).astype(jnp.bfloat16)
    slot_back = jnp.einsum(
        "erf,edf->erd", gate_grad, gate_matrix, preferred_element_type=jnp.float32
    )
    slot_back = slot_back + jnp.einsum(
        "erf,edf->erd", up_grad, up_matrix, preferred_element_type=jnp.float32
    )
    return (slot_back.astype(jnp.bfloat16), weight_grad)


def routed_body(
    forward_input,
    queries,
    new_keys,
    new_values,
    cache_keys,
    cache_values,
    context_lengths,
    norm_gain,
    router,
    gate_weight,
    up_weight,
    down_weight,
    forward_ids,
    backward_input,
    backward_ids,
    output_grad,
):
    tokens = forward_input.shape[1]
    experts = router.shape[2]
    fan_out = forward_ids.shape[2]
    per_device = gate_weight.shape[1]
    sources = lax.axis_size("expert")
    capacity = max(2, tokens * fan_out // experts + max(1, tokens * fan_out // (8 * experts)))
    gain = norm_gain[0]
    table = router[0]
    gate_local = gate_weight[0]
    up_local = up_weight[0]
    down_local = down_weight[0]
    mixed = attention(
        queries[0],
        new_keys[0],
        new_values[0],
        cache_keys[0],
        cache_values[0],
        context_lengths[0, 0],
    )
    resid_ahead = (forward_input[0].astype(jnp.float32) + mixed.astype(jnp.float32)).astype(
        jnp.bfloat16
    )
    ahead_wide, ahead_inv, ahead_normed = normalize(resid_ahead, gain)
    ahead_probs, ahead_selects = routing(ahead_normed, forward_ids[0], table)
    ahead_target = place_slots(ahead_selects, capacity)
    ahead_buffer = pack_rows(ahead_normed, ahead_target, experts, capacity)
    behind_wide, behind_inv, behind_normed = normalize(backward_input[0], gain)
    behind_probs, behind_selects = routing(behind_normed, backward_ids[0], table)
    behind_target = place_slots(behind_selects, capacity)
    rows_buffer = pack_rows(behind_normed, behind_target, experts, capacity)
    grads_buffer = pack_rows(output_grad[0], behind_target, experts, capacity)
    arrived = lax.all_to_all(ahead_buffer, "expert", split_axis=0, concat_axis=0, tiled=True)
    produced = scatter_slots(
        expert_ahead(gather_slots(arrived, per_device), gate_local, up_local, down_local), sources
    )
    returned, behind_rows, behind_grads = (
        lax.all_to_all(produced, "expert", split_axis=0, concat_axis=0, tiled=True),
        lax.all_to_all(rows_buffer, "expert", split_axis=0, concat_axis=0, tiled=True),
        lax.all_to_all(grads_buffer, "expert", split_axis=0, concat_axis=0, tiled=True),
    )
    slot_back, slot_weight = expert_behind(
        gather_slots(behind_rows, per_device),
        gather_slots(behind_grads, per_device),
        gate_local,
        up_local,
        down_local,
    )
    input_back, weight_back = (
        lax.all_to_all(
            scatter_slots(slot_back, sources), "expert", split_axis=0, concat_axis=0, tiled=True
        ),
        lax.all_to_all(
            scatter_slots(slot_weight, sources), "expert", split_axis=0, concat_axis=0, tiled=True
        ),
    )
    ahead_rows = unpack_rows(returned, ahead_target).astype(jnp.float32)
    ahead_output = (ahead_wide + jnp.sum(ahead_probs[:, :, None] * ahead_rows, axis=1)).astype(
        jnp.bfloat16
    )
    input_rows = unpack_rows(input_back, behind_target).astype(jnp.float32)
    weight_rows = weight_back.reshape(-1)[behind_target].astype(jnp.float32)
    normed_grad = jnp.sum(behind_probs[:, :, None] * input_rows, axis=1)
    logit_terms = behind_probs * (
        weight_rows - jnp.sum(behind_probs * weight_rows, axis=-1, keepdims=True)
    )
    logit_grad = jnp.sum(jnp.where(behind_selects, logit_terms[:, :, None], 0.0), axis=1).astype(
        jnp.bfloat16
    )
    normed_grad = normed_grad + jnp.dot(logit_grad, table.T, preferred_element_type=jnp.float32)
    grad_factor = (tokens * sources) ** (-0.5)
    router_term = (
        jnp.dot(behind_normed.T, logit_grad, preferred_element_type=jnp.float32) * grad_factor
    )
    scaled_grad = normed_grad * gain
    resid_grad = behind_inv * (
        scaled_grad
        - behind_wide
        * behind_inv
        * behind_inv
        * jnp.mean(scaled_grad * behind_wide, axis=-1, keepdims=True)
    )
    gain_term = jnp.sum(normed_grad * behind_wide * behind_inv, axis=0) * grad_factor
    input_grad = (output_grad[0].astype(jnp.float32) + resid_grad).astype(jnp.bfloat16)
    router_part, gain_part = (
        lax.psum_scatter(router_term, "expert", scatter_dimension=0, tiled=True),
        lax.psum_scatter(gain_term, "expert", scatter_dimension=0, tiled=True),
    )
    crossing = extended(jnp.stack([input_grad, ahead_output]), (("pipe", 0),), 1)
    return (crossing[0][None], crossing[3][None], router_part[None], gain_part[None])


def shares(normed, expert_ids, table):
    logits = jnp.dot(normed, table, preferred_element_type=jnp.float32)
    selects = expert_ids[:, :, None] == jnp.arange(table.shape[1], dtype=jnp.int32)
    chosen = jnp.any(selects, axis=1)
    top = jnp.max(jnp.where(chosen, logits, far_below), axis=-1, keepdims=True)
    lifted = jnp.where(chosen, jnp.exp(logits - top), 0.0)
    return lifted / jnp.sum(lifted, axis=-1, keepdims=True)


def dense_body(
    forward_input,
    queries,
    new_keys,
    new_values,
    cache_keys,
    cache_values,
    context_lengths,
    norm_gain,
    router,
    gate_weight,
    up_weight,
    down_weight,
    forward_ids,
    backward_input,
    backward_ids,
    output_grad,
):
    tokens = forward_input.shape[1]
    sources = lax.axis_size("expert")
    mine = lax.axis_index("expert")
    gain = norm_gain[0]
    table = router[0]
    gate_local = gate_weight[0]
    up_local = up_weight[0]
    down_local = down_weight[0]

    def everyone(rows):
        return lax.all_gather(rows, "expert", axis=0, tiled=True)

    def own_column(probs):
        every = lax.all_gather(probs, "expert", axis=0, tiled=True)
        return lax.dynamic_slice_in_dim(every, mine, 1, axis=1)

    all_grads = everyone(output_grad[0])
    behind_wide, behind_inv, behind_normed = normalize(backward_input[0], gain)
    all_behind = everyone(behind_normed)
    behind_probs = shares(behind_normed, backward_ids[0], table)
    mixed = attention(
        queries[0],
        new_keys[0],
        new_values[0],
        cache_keys[0],
        cache_values[0],
        context_lengths[0, 0],
    )
    resid_ahead = (forward_input[0].astype(jnp.float32) + mixed.astype(jnp.float32)).astype(
        jnp.bfloat16
    )
    ahead_wide, ahead_inv, ahead_normed = normalize(resid_ahead, gain)
    all_ahead = everyone(ahead_normed)
    ahead_probs = shares(ahead_normed, forward_ids[0], table)
    both = own_column(jnp.concatenate([behind_probs, ahead_probs], axis=0))
    both = both.reshape(sources, 2, tokens, 1)
    behind_share = both[:, 0].reshape(-1, 1)
    ahead_share = both[:, 1].reshape(-1, 1)
    slot_back, slot_weight = expert_behind(
        all_behind[None], all_grads[None], gate_local, up_local, down_local
    )
    back = (slot_back[0].astype(jnp.float32) * behind_share).astype(jnp.bfloat16)
    back_sum = lax.psum_scatter(back, "expert", scatter_dimension=0, tiled=True)
    weight_rows = lax.all_to_all(
        slot_weight.reshape(sources, tokens), "expert", split_axis=0, concat_axis=0, tiled=True
    ).T.astype(jnp.float32)
    produced = expert_ahead(all_ahead[None], gate_local, up_local, down_local)
    ahead = (produced[0].astype(jnp.float32) * ahead_share).astype(jnp.bfloat16)
    ahead_sum = lax.psum_scatter(ahead, "expert", scatter_dimension=0, tiled=True)
    ahead_output = (ahead_wide + ahead_sum.astype(jnp.float32)).astype(jnp.bfloat16)
    logit_grad = (
        behind_probs
        * (weight_rows - jnp.sum(behind_probs * weight_rows, axis=-1, keepdims=True))
    ).astype(jnp.bfloat16)
    normed_grad = back_sum.astype(jnp.float32) + jnp.dot(
        logit_grad, table.T, preferred_element_type=jnp.float32
    )
    grad_factor = (tokens * sources) ** (-0.5)
    router_term = (
        jnp.dot(behind_normed.T, logit_grad, preferred_element_type=jnp.float32) * grad_factor
    )
    scaled_grad = normed_grad * gain
    resid_grad = behind_inv * (
        scaled_grad
        - behind_wide
        * behind_inv
        * behind_inv
        * jnp.mean(scaled_grad * behind_wide, axis=-1, keepdims=True)
    )
    gain_term = jnp.sum(normed_grad * behind_wide * behind_inv, axis=0) * grad_factor
    input_grad = (output_grad[0].astype(jnp.float32) + resid_grad).astype(jnp.bfloat16)
    router_part, gain_part = (
        lax.psum_scatter(router_term, "expert", scatter_dimension=0, tiled=True),
        lax.psum_scatter(gain_term, "expert", scatter_dimension=0, tiled=True),
    )
    crossing = extended(jnp.stack([input_grad, ahead_output]), (("pipe", 0),), 1)
    return (crossing[0][None], crossing[3][None], router_part[None], gain_part[None])


def body(*operands):
    experts, fan_out = (operands[8].shape[2], operands[12].shape[2])
    one_each = experts == lax.axis_size("expert")
    return (dense_body if one_each and experts <= 2 * fan_out else routed_body)(*operands)


def solution(mesh):
    placed = (
        P("pipe", "expert", None),
        P("pipe", "expert", None),
        P("pipe", "expert", None),
        P("pipe", "expert", None),
        P("pipe", "expert", None),
        P("pipe", "expert", None),
        P("pipe", "expert"),
        P("pipe", None),
        P("pipe", None, None),
        P("pipe", "expert", None, None),
        P("pipe", "expert", None, None),
        P("pipe", "expert", None, None),
        P("pipe", "expert", None),
        P("pipe", "expert", None),
        P("pipe", "expert", None),
        P("pipe", "expert", None),
    )
    return jax.shard_map(
        body,
        mesh=mesh,
        in_specs=placed,
        out_specs=(
            P("pipe", "expert", None),
            P("pipe", "expert", None),
            P("pipe", "expert", None),
            P("pipe", "expert"),
        ),
        check_vma=False,
    )
```

```python
import jax
import jax.numpy as jnp
from jax import lax
from jax.experimental import pallas as pl
from jax.experimental.pallas import tpu as pltpu
from jax.sharding import PartitionSpec as P

HEADS = 16
KV_HEADS = 2
HEAD_DIM = 128


epsilon = 1e-06
far_below = -1e30


def extended(x, sides, width):
    for axis, dim in sides:
        devices, length = (lax.axis_size(axis), x.shape[dim])
        up = [(i, (i + 1) % devices) for i in range(devices)]
        down = [(j, i) for i, j in up]
        last = lax.slice_in_dim(x, length - width, length, axis=dim)
        leading = lax.slice_in_dim(x, 0, width, axis=dim)
        before = lax.ppermute(last, axis, up)
        after = lax.ppermute(leading, axis, down)
        x = jnp.concatenate([before, x, after], axis=dim)
    return x


def normalize(resid, gain):
    wide = resid.astype(jnp.float32)
    inv_rms = lax.rsqrt(jnp.mean(wide * wide, axis=-1, keepdims=True) + epsilon)
    return (wide, inv_rms, (wide * inv_rms * gain).astype(jnp.bfloat16))


def routing(normed, expert_ids, table):
    logits = jnp.dot(normed, table, preferred_element_type=jnp.float32)
    selects = expert_ids[:, :, None] == jnp.arange(table.shape[1], dtype=jnp.int32)
    chosen = jnp.sum(jnp.where(selects, logits[:, None, :], 0.0), axis=-1)
    route_probs = 1.0 / jnp.sum(jnp.exp(chosen[:, None, :] - chosen[:, :, None]), axis=-1)
    return (route_probs, selects)


def place_slots(selects, capacity):
    counted = selects.reshape(-1, selects.shape[-1]).astype(jnp.int32)
    running = jnp.cumsum(counted, axis=0)
    slot_index = jnp.sum(counted * running, axis=-1) - 1
    owner = jnp.sum(counted * jnp.arange(selects.shape[-1], dtype=jnp.int32), axis=-1)
    return (owner * capacity + slot_index).reshape(selects.shape[0], selects.shape[1])


def pack_rows(source_rows, target, experts, capacity):
    buffer = jnp.zeros((experts * capacity, source_rows.shape[1]), source_rows.dtype)
    spread = jnp.broadcast_to(source_rows[:, None, :], target.shape + (source_rows.shape[1],))
    return buffer.at[target].set(spread).reshape(experts, capacity, source_rows.shape[1])


def unpack_rows(buffer, target):
    return buffer.reshape((-1,) + buffer.shape[2:])[target]


def gather_slots(received, per_device):
    shaped = received.reshape((-1, per_device) + received.shape[1:])
    return jnp.swapaxes(shaped, 0, 1).reshape((per_device, -1) + received.shape[2:])


def scatter_slots(result, sources):
    shaped = result.reshape((result.shape[0], sources, -1) + result.shape[2:])
    return jnp.swapaxes(shaped, 0, 1).reshape((-1,) + shaped.shape[2:])


def attention(queries, new_keys, new_values, cache_keys, cache_values, length):
    tokens = queries.shape[0]
    context = cache_keys.shape[0]
    key_rows = jnp.concatenate([cache_keys, new_keys], axis=0).reshape(-1, KV_HEADS, HEAD_DIM)
    value_rows = jnp.concatenate([cache_values, new_values], axis=0).reshape(-1, KV_HEADS, HEAD_DIM)
    grouped = queries.reshape(tokens, KV_HEADS, HEADS // KV_HEADS, HEAD_DIM)
    scores = jnp.einsum(
        "tkgd,skd->kgts", grouped, key_rows, preferred_element_type=jnp.float32
    ) * HEAD_DIM ** (-0.5)
    position = jnp.arange(key_rows.shape[0], dtype=jnp.int32)[None, :]
    query_pos = jnp.arange(tokens, dtype=jnp.int32)[:, None]
    visible = jnp.where(position < context, position < length, position - context <= query_pos)
    scores = jnp.where(visible, scores, far_below)
    row_max = jnp.max(scores, axis=-1, keepdims=True)
    lifted = jnp.exp(scores - row_max)
    attn_weights = (lifted / jnp.sum(lifted, axis=-1, keepdims=True)).astype(jnp.bfloat16)
    merged = jnp.einsum(
        "kgts,skd->tkgd", attn_weights, value_rows, preferred_element_type=jnp.float32
    )
    return merged.reshape(tokens, HEADS * HEAD_DIM).astype(jnp.bfloat16)


def expert_ahead(slot_rows, gate_matrix, up_matrix, down_matrix):
    gate_pre = jnp.einsum(
        "erd,edf->erf", slot_rows, gate_matrix, preferred_element_type=jnp.float32
    )
    up_pre = jnp.einsum("erd,edf->erf", slot_rows, up_matrix, preferred_element_type=jnp.float32)
    hidden = (gate_pre * jax.nn.sigmoid(gate_pre) * up_pre).astype(jnp.bfloat16)
    return jnp.einsum(
        "erf,efd->erd", hidden, down_matrix, preferred_element_type=jnp.float32
    ).astype(jnp.bfloat16)


def expert_behind(slot_rows, slot_grads, gate_matrix, up_matrix, down_matrix):
    gate_pre = jnp.einsum(
        "erd,edf->erf", slot_rows, gate_matrix, preferred_element_type=jnp.float32
    )
    up_pre = jnp.einsum("erd,edf->erf", slot_rows, up_matrix, preferred_element_type=jnp.float32)
    sigmoid_gate = jax.nn.sigmoid(gate_pre)
    gate_act = gate_pre * sigmoid_gate
    hidden = (gate_act * up_pre).astype(jnp.bfloat16)
    down_grad = jnp.einsum(
        "erd,efd->erf", slot_grads, down_matrix, preferred_element_type=jnp.float32
    )
    weight_grad = jnp.sum(hidden.astype(jnp.float32) * down_grad, axis=-1).astype(jnp.bfloat16)
    slope_act = sigmoid_gate * (1.0 + gate_pre * (1.0 - sigmoid_gate))
    gate_grad = (down_grad * up_pre * slope_act).astype(jnp.bfloat16)
    up_grad = (down_grad * gate_act).astype(jnp.bfloat16)
    slot_back = jnp.einsum(
        "erf,edf->erd", gate_grad, gate_matrix, preferred_element_type=jnp.float32
    )
    slot_back = slot_back + jnp.einsum(
        "erf,edf->erd", up_grad, up_matrix, preferred_element_type=jnp.float32
    )
    return (slot_back.astype(jnp.bfloat16), weight_grad)


def routed_body(
    forward_input,
    queries,
    new_keys,
    new_values,
    cache_keys,
    cache_values,
    context_lengths,
    norm_gain,
    router,
    gate_weight,
    up_weight,
    down_weight,
    forward_ids,
    backward_input,
    backward_ids,
    output_grad,
):
    tokens = forward_input.shape[1]
    experts = router.shape[2]
    fan_out = forward_ids.shape[2]
    per_device = gate_weight.shape[1]
    sources = lax.axis_size("expert")
    capacity = max(2, tokens * fan_out // experts + max(1, tokens * fan_out // (8 * experts)))
    gain = norm_gain[0]
    table = router[0]
    gate_local = gate_weight[0]
    up_local = up_weight[0]
    down_local = down_weight[0]
    mixed = attention(
        queries[0],
        new_keys[0],
        new_values[0],
        cache_keys[0],
        cache_values[0],
        context_lengths[0, 0],
    )
    resid_ahead = (forward_input[0].astype(jnp.float32) + mixed.astype(jnp.float32)).astype(
        jnp.bfloat16
    )
    ahead_wide, ahead_inv, ahead_normed = normalize(resid_ahead, gain)
    ahead_probs, ahead_selects = routing(ahead_normed, forward_ids[0], table)
    ahead_target = place_slots(ahead_selects, capacity)
    ahead_buffer = pack_rows(ahead_normed, ahead_target, experts, capacity)
    behind_wide, behind_inv, behind_normed = normalize(backward_input[0], gain)
    behind_probs, behind_selects = routing(behind_normed, backward_ids[0], table)
    behind_target = place_slots(behind_selects, capacity)
    rows_buffer = pack_rows(behind_normed, behind_target, experts, capacity)
    grads_buffer = pack_rows(output_grad[0], behind_target, experts, capacity)
    arrived = lax.all_to_all(ahead_buffer, "expert", split_axis=0, concat_axis=0, tiled=True)
    produced = scatter_slots(
        expert_ahead(gather_slots(arrived, per_device), gate_local, up_local, down_local), sources
    )
    returned, behind_rows, behind_grads = (
        lax.all_to_all(produced, "expert", split_axis=0, concat_axis=0, tiled=True),
        lax.all_to_all(rows_buffer, "expert", split_axis=0, concat_axis=0, tiled=True),
        lax.all_to_all(grads_buffer, "expert", split_axis=0, concat_axis=0, tiled=True),
    )
    slot_back, slot_weight = expert_behind(
        gather_slots(behind_rows, per_device),
        gather_slots(behind_grads, per_device),
        gate_local,
        up_local,
        down_local,
    )
    input_back, weight_back = (
        lax.all_to_all(
            scatter_slots(slot_back, sources), "expert", split_axis=0, concat_axis=0, tiled=True
        ),
        lax.all_to_all(
            scatter_slots(slot_weight, sources), "expert", split_axis=0, concat_axis=0, tiled=True
        ),
    )
    ahead_rows = unpack_rows(returned, ahead_target).astype(jnp.float32)
    ahead_output = (ahead_wide + jnp.sum(ahead_probs[:, :, None] * ahead_rows, axis=1)).astype(
        jnp.bfloat16
    )
    input_rows = unpack_rows(input_back, behind_target).astype(jnp.float32)
    weight_rows = weight_back.reshape(-1)[behind_target].astype(jnp.float32)
    normed_grad = jnp.sum(behind_probs[:, :, None] * input_rows, axis=1)
    logit_terms = behind_probs * (
        weight_rows - jnp.sum(behind_probs * weight_rows, axis=-1, keepdims=True)
    )
    logit_grad = jnp.sum(jnp.where(behind_selects, logit_terms[:, :, None], 0.0), axis=1).astype(
        jnp.bfloat16
    )
    normed_grad = normed_grad + jnp.dot(logit_grad, table.T, preferred_element_type=jnp.float32)
    grad_factor = (tokens * sources) ** (-0.5)
    router_term = (
        jnp.dot(behind_normed.T, logit_grad, preferred_element_type=jnp.float32) * grad_factor
    )
    scaled_grad = normed_grad * gain
    resid_grad = behind_inv * (
        scaled_grad
        - behind_wide
        * behind_inv
        * behind_inv
        * jnp.mean(scaled_grad * behind_wide, axis=-1, keepdims=True)
    )
    gain_term = jnp.sum(normed_grad * behind_wide * behind_inv, axis=0) * grad_factor
    input_grad = (output_grad[0].astype(jnp.float32) + resid_grad).astype(jnp.bfloat16)
    router_part, gain_part = (
        lax.psum_scatter(router_term, "expert", scatter_dimension=0, tiled=True),
        lax.psum_scatter(gain_term, "expert", scatter_dimension=0, tiled=True),
    )
    crossing = extended(jnp.stack([input_grad, ahead_output]), (("pipe", 0),), 1)
    return (crossing[0][None], crossing[3][None], router_part[None], gain_part[None])


TILE = 256
SUB = 2
VMEM_LIMIT = 60 * 2**20


def fits(operands):
    experts, fan_out = (operands[8].shape[2], operands[12].shape[2])
    tokens, width = operands[0].shape[1:]
    hidden = operands[9].shape[3]
    return (
        lax.axis_size("expert") == 2**3
        and experts == lax.axis_size("expert")
        and experts <= 2 * fan_out
        and lax.axis_size("pipe") > 1
        and tokens == HEAD_DIM
        and operands[4].shape[1] == tokens
        and width % TILE == 0
        and hidden % TILE == 0
    )


def section_kernel(
    length_ref,
    fin_ref,
    q_ref,
    nk_ref,
    nv_ref,
    ck_ref,
    cv_ref,
    gain_ref,
    router_ref,
    gate_ref,
    up_ref,
    down_ref,
    fids_ref,
    bin_ref,
    bids_ref,
    og_ref,
    out_fwd,
    out_back,
    out_sums,
    gat,
    gate_v,
    up_v,
    down_v,
    part,
    sibr,
    rx,
    act_a,
    act_b,
    wacc,
    pcol,
    ptab,
    wgs,
    wgr,
    rgp,
    rgr,
    x_v,
    fin_v,
    q_v,
    k_v,
    v_v,
    resid_v,
    staged,
    table,
    lg_rows,
    gacc,
    local_sem,
    gsend,
    grecv,
    ssend,
    srecv,
    xsend,
    xrecv,
    zsend,
    zrecv,
    tsend,
    trecv,
):
    tokens, width = fin_ref.shape
    hidden_tiles = gate_v.shape[0]
    wide_tiles = width // TILE
    half = tokens // 2
    small = half // SUB
    experts = ptab.shape[2]
    group = ptab.shape[1]
    heads = width // HEAD_DIM
    f32, bf16 = jnp.float32, jnp.bfloat16
    nt = (((1,), (1,)), ((), ()))

    me = lax.axis_index("expert")
    core, at_x, at_y = me % 2, (me // 2) % 2, me // 4
    pipe, pipes = lax.axis_index("pipe"), lax.axis_size("pipe")
    following, previous = (pipe + 1) % pipes, (pipe + pipes - 1) % pipes

    def peer(j):
        a = 1 - core if j % 2 else core
        b = 1 - at_x if (j // 2) % 2 else at_x
        c = 1 - at_y if j // 4 else at_y
        return (c * 2 + b) * 2 + a

    def at(j):
        return {"expert": peer(j)}

    SIB, XN, YN = 1, 2, 4

    def remote(src, dst, send, recv, where):
        return pltpu.make_async_remote_copy(
            src_ref=src,
            dst_ref=dst,
            send_sem=send,
            recv_sem=recv,
            device_id=where,
            device_id_type=pl.DeviceIdType.MESH,
        )

    gather_plan = (
        (0, 0, 0, tokens, tokens, SIB),
        (0, 0, 1, 0, half, XN),
        (0, half, 1, half, half, XN),
        (0, half, 2, half, half, YN),
        (0, 0, 2, 0, half, YN),
        (1, 0, 3, 0, half, YN),
        (2, half, 3, half, half, XN),
        (1, 0, 1, tokens, half, SIB),
        (1, half, 1, tokens + half, half, SIB),
        (2, 0, 2, tokens, half, SIB),
        (2, half, 2, tokens + half, half, SIB),
        (3, 0, 3, tokens, half, SIB),
        (3, half, 3, tokens + half, half, SIB),
    )

    def gcopy(a, i):
        sb, sr, tb, tr, rows, j = gather_plan[i]
        return remote(
            gat.at[a, sb, pl.ds(sr, rows)],
            gat.at[a, tb, pl.ds(tr, rows)],
            gsend.at[a, i],
            grecv.at[a, i],
            at(j),
        )

    def scopy(m, r):
        return remote(
            part.at[m, r, pl.ds(tokens, tokens)],
            sibr.at[m, r],
            ssend.at[m, r],
            srecv.at[m, r],
            at(SIB),
        )

    reduce_plan = ((3, 0, XN), (1, 0, XN), (1, half, XN), (3, half, YN), (2, half, YN), (2, 0, YN))

    def xcopy(m, k, q):
        r, row, j = reduce_plan[k]
        return remote(
            part.at[m, r, pl.ds(row + q * small, small)],
            rx.at[m, k, pl.ds(q * small, small)],
            xsend.at[m, k, q],
            xrecv.at[m, k, q],
            at(j),
        )

    def zcopy(m, i):
        rows = pl.ds(i * small, small)
        out, there = (out_fwd, following) if m else (out_back, previous)
        return remote(
            staged.at[m, rows], out.at[rows], zsend.at[m, i], zrecv.at[m, i], {"pipe": there}
        )

    def tcopy(kind, j):
        src, dst = (
            (ptab.at[0, 0], ptab.at[0, j]),
            (ptab.at[1, 0], ptab.at[1, j]),
            (wgs.at[j], wgr.at[j]),
            (rgp.at[peer(j)], rgr.at[j]),
        )[kind]
        return remote(src, dst, tsend.at[kind, j], trecv.at[kind, j], at(j))

    loads = [
        (og_ref, gat.at[0, 0, pl.ds(0, tokens)]),
        (bin_ref, x_v),
        (q_ref, q_v),
        (ck_ref, k_v.at[pl.ds(0, tokens)]),
        (nk_ref, k_v.at[pl.ds(tokens, tokens)]),
        (cv_ref, v_v.at[pl.ds(0, tokens)]),
        (nv_ref, v_v.at[pl.ds(tokens, tokens)]),
        (fin_ref, fin_v),
    ]
    for t in range(hidden_tiles):
        cols = pl.ds(t * TILE, TILE)
        loads += [
            (gate_ref.at[:, cols], gate_v.at[t]),
            (up_ref.at[:, cols], up_v.at[t]),
            (down_ref.at[cols], down_v.at[t]),
        ]
    loads = [
        pltpu.make_async_copy(src, dst, local_sem.at[i]) for i, (src, dst) in enumerate(loads)
    ]
    for copy in loads:
        copy.start()

    barrier = pltpu.get_barrier_semaphore()
    for j in range(1, group):
        pl.semaphore_signal(barrier, inc=1, device_id=at(j), device_id_type=pl.DeviceIdType.MESH)
    for there in (following, previous):
        pl.semaphore_signal(
            barrier, inc=1, device_id={"pipe": there}, device_id_type=pl.DeviceIdType.MESH
        )
    pl.semaphore_wait(barrier, group - 1 + 2)

    loads[0].wait()
    for i in (1, 3, 2, 4, 0):
        gcopy(0, i).start()

    table[...] = jnp.zeros_like(table)
    table[0 : router_ref.shape[0], :] = router_ref[...]
    gain = gain_ref[...]

    def normalize_rows(source, a):
        def step(i, carry):
            rows = pl.ds(pl.multiple_of(i * 32, 32), 32)
            x = source[rows, :].astype(f32)
            inv = lax.rsqrt(jnp.mean(x * x, axis=-1, keepdims=True) + epsilon)
            gat[a, 0, rows, :] = (x * inv * gain_ref[...]).astype(bf16)
            return carry

        lax.fori_loop(0, tokens // 32, step, 0)

    expert_row = lax.broadcasted_iota(jnp.int32, (experts, tokens), 0)

    def chosen_mask(ids_ref):
        ids = ids_ref[...]
        mask = ids[0:1, :] == expert_row
        for k in range(1, ids.shape[0]):
            mask = mask | (ids[k : k + 1, :] == expert_row)
        return mask

    def route(a, ids_ref, m):
        logits = lax.dot_general(
            table[...], gat[a, 0, 0:tokens, :], nt, preferred_element_type=f32
        )[0:experts, :]
        mask = chosen_mask(ids_ref)
        top = jnp.max(jnp.where(mask, logits, far_below), axis=0, keepdims=True)
        lifted = jnp.where(mask, jnp.exp(jnp.where(mask, logits - top, 0.0)), 0.0)
        ptab[m, 0] = lifted / jnp.sum(lifted, axis=0, keepdims=True)

    loads[1].wait()
    normalize_rows(x_v, 1)
    for i in (1, 3, 2, 4, 0):
        gcopy(1, i).start()
    route(1, bids_ref, 0)
    for j in range(1, group):
        tcopy(0, j).start()

    for i in range(2, 8):
        loads[i].wait()
    length = length_ref[0, 0]

    def one_head(h, carry):
        cols = pl.ds(pl.multiple_of(h * HEAD_DIM, HEAD_DIM), HEAD_DIM)
        shared = h // (HEADS // KV_HEADS)
        kv_cols = pl.ds(pl.multiple_of(shared * HEAD_DIM, HEAD_DIM), HEAD_DIM)
        scores = lax.dot_general(
            q_v[:, cols], k_v[:, kv_cols], nt, preferred_element_type=f32
        ) * HEAD_DIM ** (-0.5)
        position = lax.broadcasted_iota(jnp.int32, scores.shape, 1)
        query_pos = lax.broadcasted_iota(jnp.int32, scores.shape, 0)
        visible = ((position < tokens) & (position < length)) | (
            (position >= tokens) & (position - tokens <= query_pos)
        )
        scores = jnp.where(visible, scores, far_below)
        lifted = jnp.exp(scores - jnp.max(scores, axis=-1, keepdims=True))
        weights = (lifted / jnp.sum(lifted, axis=-1, keepdims=True)).astype(bf16)
        mixed = jnp.dot(weights, v_v[:, kv_cols], preferred_element_type=f32).astype(bf16)
        resid_v[:, cols] = (fin_v[:, cols].astype(f32) + mixed.astype(f32)).astype(bf16)
        return carry

    lax.fori_loop(0, heads, one_head, 0)
    normalize_rows(resid_v, 2)
    route(2, fids_ref, 1)
    for j in range(1, group):
        tcopy(1, j).start()
    for copy in loads[8:]:
        copy.wait()
    for kind in (0, 1):
        for j in range(1, group):
            tcopy(kind, j).wait_recv()

    def share_column(m, r):
        for s in range(2):
            row = jnp.sum(jnp.where(expert_row == me, ptab[m, 2 * r + s], 0.0), axis=0, keepdims=True)
            pcol[s * tokens : (s + 1) * tokens, :] = jnp.broadcast_to(row, (tokens, tokens)).T

    def behind_block(r):
        wacc[...] = jnp.zeros_like(wacc)

        def tile(t, carry):
            rows = gat[1, r]
            gate_pre = jnp.dot(rows, gate_v[t], preferred_element_type=f32)
            up_pre = jnp.dot(rows, up_v[t], preferred_element_type=f32)
            down_grad = lax.dot_general(gat[0, r], down_v[t], nt, preferred_element_type=f32)
            sig = jax.nn.sigmoid(gate_pre)
            gate_act = gate_pre * sig
            weighed = (gate_act * up_pre).astype(bf16).astype(f32) * down_grad
            folded = weighed[:, 0:tokens]
            for c in range(1, TILE // tokens):
                folded = folded + weighed[:, c * tokens : (c + 1) * tokens]
            wacc[...] += folded
            slope = sig * (1.0 + gate_pre * (1.0 - sig))
            act_a[t] = (down_grad * up_pre * slope).astype(bf16)
            act_b[t] = (down_grad * gate_act).astype(bf16)
            return carry

        lax.fori_loop(0, hidden_tiles, tile, 0)
        for s in range(2):
            row = jnp.sum(wacc[s * tokens : (s + 1) * tokens, :].T, axis=0, keepdims=True)
            wgs[2 * r + s] = jnp.where(expert_row == me, row, 0.0)
        share_column(0, r)

        def back(n, carry):
            cols = pl.ds(pl.multiple_of(n * TILE, TILE), TILE)
            total = jnp.zeros((2 * tokens, TILE), f32)
            for t in range(hidden_tiles):
                total += lax.dot_general(act_a[t], gate_v[t, cols, :], nt, preferred_element_type=f32)
                total += lax.dot_general(act_b[t], up_v[t, cols, :], nt, preferred_element_type=f32)
            part[0, r, :, cols] = (total * pcol[:, 0:1]).astype(bf16)
            return carry

        lax.fori_loop(0, wide_tiles, back, 0)

    def ahead_block(r):
        def tile(t, carry):
            rows = gat[2, r]
            gate_pre = jnp.dot(rows, gate_v[t], preferred_element_type=f32)
            up_pre = jnp.dot(rows, up_v[t], preferred_element_type=f32)
            act_a[t] = (gate_pre * jax.nn.sigmoid(gate_pre) * up_pre).astype(bf16)
            return carry

        lax.fori_loop(0, hidden_tiles, tile, 0)
        share_column(1, r)

        def out(n, carry):
            cols = pl.ds(pl.multiple_of(n * TILE, TILE), TILE)
            total = jnp.zeros((2 * tokens, TILE), f32)
            for t in range(hidden_tiles):
                total += jnp.dot(act_a[t], down_v[t, :, cols], preferred_element_type=f32)
            part[1, r, :, cols] = (total * pcol[:, 0:1]).astype(bf16)
            return carry

        lax.fori_loop(0, wide_tiles, out, 0)

    def add_rows(m, r, base, count, other, other_base):
        def step(i, carry):
            to = pl.ds(pl.multiple_of(base + i * 32, 32), 32)
            since = pl.ds(pl.multiple_of(other_base + i * 32, 32), 32)
            part[m, r, to, :] = (
                part[m, r, to, :].astype(f32) + other[since, :].astype(f32)
            ).astype(bf16)
            return carry

        lax.fori_loop(0, count // 32, step, 0)

    def join_sibling(m, r):
        scopy(m, r).wait_recv()
        add_rows(m, r, 0, tokens, sibr.at[m, r], 0)

    def first_phase(m):
        join_sibling(m, 3)
        for q in range(SUB):
            xcopy(m, 0, q).start()
            xcopy(m, 3, q).start()
        join_sibling(m, 1)
        for q in range(SUB):
            xcopy(m, 1, q).start()
        join_sibling(m, 2)
        for q in range(SUB):
            xcopy(m, 4, q).start()
        join_sibling(m, 0)

    def second_phase(m):
        for q in range(SUB):
            xcopy(m, 0, q).wait_recv()
            add_rows(m, 2, q * small, small, rx.at[m, 0], q * small)
            xcopy(m, 5, q).start()
            xcopy(m, 3, q).wait_recv()
            add_rows(m, 1, half + q * small, small, rx.at[m, 3], q * small)
            xcopy(m, 2, q).start()

    def forward_first(a):
        gcopy(a, 1).wait_recv()
        gcopy(a, 5).start()
        gcopy(a, 7).start()
        gcopy(a, 3).wait_recv()
        gcopy(a, 6).start()
        gcopy(a, 10).start()

    def forward_second(a):
        gcopy(a, 2).wait_recv()
        gcopy(a, 8).start()
        gcopy(a, 4).wait_recv()
        gcopy(a, 9).start()

    def forward_third(a):
        gcopy(a, 5).wait_recv()
        gcopy(a, 11).start()
        gcopy(a, 6).wait_recv()
        gcopy(a, 12).start()

    def arrived(a, *which):
        for i in which:
            gcopy(a, i).wait_recv()

    forward_first(0)

    def stage(step, carry):
        @pl.when(step == 0)
        def _():
            arrived(0, 0)
            arrived(1, 0)

        @pl.when(step == 1)
        def _():
            forward_second(0)
            forward_first(1)
            forward_second(1)
            for i in (1, 3, 2, 4, 0):
                gcopy(2, i).start()
            arrived(0, 7, 8)
            arrived(1, 7, 8)

        @pl.when(step == 2)
        def _():
            arrived(0, 9, 10)
            arrived(1, 9, 10)

        @pl.when(step == 3)
        def _():
            forward_third(0)
            forward_third(1)
            arrived(0, 11, 12)
            arrived(1, 11, 12)

        @pl.when(step == 4)
        def _():
            for j in range(1, group):
                tcopy(2, j).start()
            forward_first(2)
            first_phase(0)
            arrived(2, 0)

        @pl.when(step == 5)
        def _():
            forward_second(2)
            arrived(2, 7, 8)

        @pl.when(step == 6)
        def _():
            arrived(2, 9, 10)

        @pl.when(step == 7)
        def _():
            second_phase(0)
            forward_third(2)
            arrived(2, 11, 12)

        @pl.when(step < 4)
        def _():
            behind_block(step)

        @pl.when(step >= 4)
        def _():
            ahead_block(step - 4)

        for s in range(8):

            @pl.when(step == s)
            def _(s=s):
                scopy(s // 4, s % 4).start()

        return carry

    lax.fori_loop(0, 8, stage, 0)
    first_phase(1)

    wrows = wgs[0]
    for j in range(1, group):
        tcopy(2, j).wait_recv()
        wrows = wrows + wgr[j]
    probs = ptab[0, 0]
    logit_grad = probs * (wrows - jnp.sum(probs * wrows, axis=0, keepdims=True))
    padded = jnp.concatenate([logit_grad, jnp.zeros((tokens - experts, tokens), f32)], axis=0)
    lg_rows[...] = padded.T.astype(bf16)
    gacc[...] = jnp.zeros_like(gacc)

    def total_rows(m, i):
        rows = pl.ds(i * small, small)
        side, q = i // SUB, i % SUB
        inner = pl.ds(q * small, small)
        near, far = (4, 2) if side else (1, 5)
        xcopy(m, near, q).wait_recv()
        xcopy(m, far, q).wait_recv()
        return rows, near, far, inner

    def finish_behind(i):
        rows, near, far, inner = total_rows(0, i)
        for u in range(small // 16):
            at_rows = pl.ds(i * small + u * 16, 16)
            sub_rows = pl.ds((i % SUB) * small + u * 16, 16)
            normed_grad = (
                part[0, 0, at_rows, :].astype(f32)
                + rx[0, near, sub_rows, :].astype(f32)
                + rx[0, far, sub_rows, :].astype(f32)
                + jnp.dot(lg_rows[at_rows, :], table[...], preferred_element_type=f32)
            )
            x = x_v[at_rows, :].astype(f32)
            inv = lax.rsqrt(jnp.mean(x * x, axis=-1, keepdims=True) + epsilon)
            scaled = normed_grad * gain_ref[...]
            slope = jnp.mean(scaled * x, axis=-1, keepdims=True)
            resid_grad = inv * (scaled - x * (inv * inv * slope))
            gacc[...] += jnp.sum(normed_grad * x * inv, axis=0, keepdims=True)
            staged[0, at_rows, :] = (
                gat[0, 0, at_rows, :].astype(f32) + resid_grad
            ).astype(bf16)
        zcopy(0, i).start()

    def finish_ahead(i):
        rows, near, far, inner = total_rows(1, i)
        total = (
            part[1, 0, rows, :].astype(f32)
            + rx[1, near, inner, :].astype(f32)
            + rx[1, far, inner, :].astype(f32)
        )
        staged[1, rows, :] = (resid_v[rows, :].astype(f32) + total).astype(bf16)
        zcopy(1, i).start()

    order = [side * SUB + q for q in range(SUB) for side in range(2)]
    for i in order:
        finish_behind(i)

    second_phase(1)
    factor = (tokens * group) ** (-0.5)
    pad_rows = rgp.shape[1]
    lg_short = padded[0:pad_rows, :].astype(bf16)
    span = rgp.shape[2]
    which = lax.broadcasted_iota(jnp.int32, (pad_rows, span), 0)
    for d in range(group):
        cols = slice(d * span, (d + 1) * span)
        grads = jnp.dot(lg_short, gat[1, 0, 0:tokens, cols], preferred_element_type=f32)
        rgp[d] = jnp.where(which == experts, gacc[:, cols], grads) * factor
    for j in range(1, group):
        tcopy(3, j).start()

    for i in order:
        finish_ahead(i)

    sums = rgp[me]
    for j in range(1, group):
        tcopy(3, j).wait_recv()
        sums = sums + rgr[j]
    out_sums[...] = sums

    for a in range(3):
        for i in range(len(gather_plan)):
            gcopy(a, i).wait_send()
    for kind in range(4):
        for j in range(1, group):
            tcopy(kind, j).wait_send()
    for m in range(2):
        for r in range(4):
            scopy(m, r).wait_send()
        for k in range(len(reduce_plan)):
            for q in range(SUB):
                xcopy(m, k, q).wait_send()
        for i in range(2 * SUB):
            zcopy(m, i).wait()


def kernel_body(
    forward_input,
    queries,
    new_keys,
    new_values,
    cache_keys,
    cache_values,
    context_lengths,
    norm_gain,
    router,
    gate_weight,
    up_weight,
    down_weight,
    forward_ids,
    backward_input,
    backward_ids,
    output_grad,
):
    tokens, width = forward_input.shape[1:]
    experts = router.shape[2]
    group = lax.axis_size("expert")
    hidden = gate_weight.shape[3]
    tiles = hidden // TILE
    pad_experts = experts + 8
    half = tokens // 2
    kv_width = cache_keys.shape[2]
    f32, bf16 = jnp.float32, jnp.bfloat16
    table = jnp.pad(router[0].T, ((0, pad_experts - experts), (0, 0)))
    hbm = pl.BlockSpec(memory_space=pl.ANY)
    near = pl.BlockSpec(memory_space=pltpu.VMEM)
    copies = 13
    dma = pltpu.SemaphoreType.DMA
    out_fwd, out_back, sums = pl.pallas_call(
        section_kernel,
        out_shape=(
            jax.ShapeDtypeStruct((tokens, width), bf16),
            jax.ShapeDtypeStruct((tokens, width), bf16),
            jax.ShapeDtypeStruct((pad_experts, width // group), f32),
        ),
        in_specs=[
            pl.BlockSpec(memory_space=pltpu.SMEM),
            hbm,
            hbm,
            hbm,
            hbm,
            hbm,
            hbm,
            near,
            near,
            hbm,
            hbm,
            hbm,
            near,
            hbm,
            near,
            hbm,
        ],
        out_specs=(hbm, hbm, near),
        scratch_shapes=[
            pltpu.VMEM((3, 4, 2 * tokens, width), bf16),
            pltpu.VMEM((tiles, width, TILE), bf16),
            pltpu.VMEM((tiles, width, TILE), bf16),
            pltpu.VMEM((tiles, TILE, width), bf16),
            pltpu.VMEM((2, 4, 2 * tokens, width), bf16),
            pltpu.VMEM((2, 4, tokens, width), bf16),
            pltpu.VMEM((2, 6, half, width), bf16),
            pltpu.VMEM((tiles, 2 * tokens, TILE), bf16),
            pltpu.VMEM((tiles, 2 * tokens, TILE), bf16),
            pltpu.VMEM((2 * tokens, tokens), f32),
            pltpu.VMEM((2 * tokens, tokens), f32),
            pltpu.VMEM((2, group, experts, tokens), f32),
            pltpu.VMEM((group, experts, tokens), f32),
            pltpu.VMEM((group, experts, tokens), f32),
            pltpu.VMEM((group, pad_experts, width // group), f32),
            pltpu.VMEM((group, pad_experts, width // group), f32),
            pltpu.VMEM((tokens, width), bf16),
            pltpu.VMEM((tokens, width), bf16),
            pltpu.VMEM((tokens, width), bf16),
            pltpu.VMEM((2 * tokens, kv_width), bf16),
            pltpu.VMEM((2 * tokens, kv_width), bf16),
            pltpu.VMEM((tokens, width), bf16),
            pltpu.VMEM((2, tokens, width), bf16),
            pltpu.VMEM((tokens, width), bf16),
            pltpu.VMEM((tokens, tokens), bf16),
            pltpu.VMEM((1, width), f32),
            dma((8 + 3 * tiles,)),
            dma((3, copies)),
            dma((3, copies)),
            dma((2, 4)),
            dma((2, 4)),
            dma((2, 6, SUB)),
            dma((2, 6, SUB)),
            dma((2, 2 * SUB)),
            dma((2, 2 * SUB)),
            dma((4, group)),
            dma((4, group)),
        ],
        compiler_params=pltpu.CompilerParams(
            collective_id=0, has_side_effects=True, vmem_limit_bytes=VMEM_LIMIT
        ),
    )(
        context_lengths,
        forward_input[0],
        queries[0],
        new_keys[0],
        new_values[0],
        cache_keys[0],
        cache_values[0],
        norm_gain,
        table,
        gate_weight[0, 0],
        up_weight[0, 0],
        down_weight[0, 0],
        forward_ids[0].T,
        backward_input[0],
        backward_ids[0].T,
        output_grad[0],
    )
    return (out_fwd[None], out_back[None], sums[:experts].T[None], sums[experts][None])


def body(*operands):
    return (kernel_body if fits(operands) else routed_body)(*operands)


def solution(mesh):
    placed = (
        P("pipe", "expert", None),
        P("pipe", "expert", None),
        P("pipe", "expert", None),
        P("pipe", "expert", None),
        P("pipe", "expert", None),
        P("pipe", "expert", None),
        P("pipe", "expert"),
        P("pipe", None),
        P("pipe", None, None),
        P("pipe", "expert", None, None),
        P("pipe", "expert", None, None),
        P("pipe", "expert", None, None),
        P("pipe", "expert", None),
        P("pipe", "expert", None),
        P("pipe", "expert", None),
        P("pipe", "expert", None),
    )
    return jax.shard_map(
        body,
        mesh=mesh,
        in_specs=placed,
        out_specs=(
            P("pipe", "expert", None),
            P("pipe", "expert", None),
            P("pipe", "expert", None),
            P("pipe", "expert"),
        ),
        check_vma=False,
    )
```

```python
import jax
import jax.numpy as jnp
from jax import lax
from jax.experimental import pallas as pl
from jax.experimental.pallas import tpu as pltpu
from jax.sharding import PartitionSpec as P

HEADS = 16
KV_HEADS = 2
HEAD_DIM = 128


epsilon = 1e-06
far_below = -1e30


def extended(x, sides, width):
    for axis, dim in sides:
        devices, length = (lax.axis_size(axis), x.shape[dim])
        up = [(i, (i + 1) % devices) for i in range(devices)]
        down = [(j, i) for i, j in up]
        last = lax.slice_in_dim(x, length - width, length, axis=dim)
        leading = lax.slice_in_dim(x, 0, width, axis=dim)
        before = lax.ppermute(last, axis, up)
        after = lax.ppermute(leading, axis, down)
        x = jnp.concatenate([before, x, after], axis=dim)
    return x


def normalize(resid, gain):
    wide = resid.astype(jnp.float32)
    inv_rms = lax.rsqrt(jnp.mean(wide * wide, axis=-1, keepdims=True) + epsilon)
    return (wide, inv_rms, (wide * inv_rms * gain).astype(jnp.bfloat16))


def routing(normed, expert_ids, table):
    logits = jnp.dot(normed, table, preferred_element_type=jnp.float32)
    selects = expert_ids[:, :, None] == jnp.arange(table.shape[1], dtype=jnp.int32)
    chosen = jnp.sum(jnp.where(selects, logits[:, None, :], 0.0), axis=-1)
    route_probs = 1.0 / jnp.sum(jnp.exp(chosen[:, None, :] - chosen[:, :, None]), axis=-1)
    return (route_probs, selects)


def place_slots(selects, capacity):
    counted = selects.reshape(-1, selects.shape[-1]).astype(jnp.int32)
    running = jnp.cumsum(counted, axis=0)
    slot_index = jnp.sum(counted * running, axis=-1) - 1
    owner = jnp.sum(counted * jnp.arange(selects.shape[-1], dtype=jnp.int32), axis=-1)
    return (owner * capacity + slot_index).reshape(selects.shape[0], selects.shape[1])


def pack_rows(source_rows, target, experts, capacity):
    buffer = jnp.zeros((experts * capacity, source_rows.shape[1]), source_rows.dtype)
    spread = jnp.broadcast_to(source_rows[:, None, :], target.shape + (source_rows.shape[1],))
    return buffer.at[target].set(spread).reshape(experts, capacity, source_rows.shape[1])


def unpack_rows(buffer, target):
    return buffer.reshape((-1,) + buffer.shape[2:])[target]


def gather_slots(received, per_device):
    shaped = received.reshape((-1, per_device) + received.shape[1:])
    return jnp.swapaxes(shaped, 0, 1).reshape((per_device, -1) + received.shape[2:])


def scatter_slots(result, sources):
    shaped = result.reshape((result.shape[0], sources, -1) + result.shape[2:])
    return jnp.swapaxes(shaped, 0, 1).reshape((-1,) + shaped.shape[2:])


def attention(queries, new_keys, new_values, cache_keys, cache_values, length):
    tokens = queries.shape[0]
    context = cache_keys.shape[0]
    key_rows = jnp.concatenate([cache_keys, new_keys], axis=0).reshape(-1, KV_HEADS, HEAD_DIM)
    value_rows = jnp.concatenate([cache_values, new_values], axis=0).reshape(-1, KV_HEADS, HEAD_DIM)
    grouped = queries.reshape(tokens, KV_HEADS, HEADS // KV_HEADS, HEAD_DIM)
    scores = jnp.einsum(
        "tkgd,skd->kgts", grouped, key_rows, preferred_element_type=jnp.float32
    ) * HEAD_DIM ** (-0.5)
    position = jnp.arange(key_rows.shape[0], dtype=jnp.int32)[None, :]
    query_pos = jnp.arange(tokens, dtype=jnp.int32)[:, None]
    visible = jnp.where(position < context, position < length, position - context <= query_pos)
    scores = jnp.where(visible, scores, far_below)
    row_max = jnp.max(scores, axis=-1, keepdims=True)
    lifted = jnp.exp(scores - row_max)
    attn_weights = (lifted / jnp.sum(lifted, axis=-1, keepdims=True)).astype(jnp.bfloat16)
    merged = jnp.einsum(
        "kgts,skd->tkgd", attn_weights, value_rows, preferred_element_type=jnp.float32
    )
    return merged.reshape(tokens, HEADS * HEAD_DIM).astype(jnp.bfloat16)


def expert_ahead(slot_rows, gate_matrix, up_matrix, down_matrix):
    gate_pre = jnp.einsum(
        "erd,edf->erf", slot_rows, gate_matrix, preferred_element_type=jnp.float32
    )
    up_pre = jnp.einsum("erd,edf->erf", slot_rows, up_matrix, preferred_element_type=jnp.float32)
    hidden = (gate_pre * jax.nn.sigmoid(gate_pre) * up_pre).astype(jnp.bfloat16)
    return jnp.einsum(
        "erf,efd->erd", hidden, down_matrix, preferred_element_type=jnp.float32
    ).astype(jnp.bfloat16)


def expert_behind(slot_rows, slot_grads, gate_matrix, up_matrix, down_matrix):
    gate_pre = jnp.einsum(
        "erd,edf->erf", slot_rows, gate_matrix, preferred_element_type=jnp.float32
    )
    up_pre = jnp.einsum("erd,edf->erf", slot_rows, up_matrix, preferred_element_type=jnp.float32)
    sigmoid_gate = jax.nn.sigmoid(gate_pre)
    gate_act = gate_pre * sigmoid_gate
    hidden = (gate_act * up_pre).astype(jnp.bfloat16)
    down_grad = jnp.einsum(
        "erd,efd->erf", slot_grads, down_matrix, preferred_element_type=jnp.float32
    )
    weight_grad = jnp.sum(hidden.astype(jnp.float32) * down_grad, axis=-1).astype(jnp.bfloat16)
    slope_act = sigmoid_gate * (1.0 + gate_pre * (1.0 - sigmoid_gate))
    gate_grad = (down_grad * up_pre * slope_act).astype(jnp.bfloat16)
    up_grad = (down_grad * gate_act).astype(jnp.bfloat16)
    slot_back = jnp.einsum(
        "erf,edf->erd", gate_grad, gate_matrix, preferred_element_type=jnp.float32
    )
    slot_back = slot_back + jnp.einsum(
        "erf,edf->erd", up_grad, up_matrix, preferred_element_type=jnp.float32
    )
    return (slot_back.astype(jnp.bfloat16), weight_grad)


def routed_body(
    forward_input,
    queries,
    new_keys,
    new_values,
    cache_keys,
    cache_values,
    context_lengths,
    norm_gain,
    router,
    gate_weight,
    up_weight,
    down_weight,
    forward_ids,
    backward_input,
    backward_ids,
    output_grad,
):
    tokens = forward_input.shape[1]
    experts = router.shape[2]
    fan_out = forward_ids.shape[2]
    per_device = gate_weight.shape[1]
    sources = lax.axis_size("expert")
    capacity = max(2, tokens * fan_out // experts + max(1, tokens * fan_out // (8 * experts)))
    gain = norm_gain[0]
    table = router[0]
    gate_local = gate_weight[0]
    up_local = up_weight[0]
    down_local = down_weight[0]
    mixed = attention(
        queries[0],
        new_keys[0],
        new_values[0],
        cache_keys[0],
        cache_values[0],
        context_lengths[0, 0],
    )
    resid_ahead = (forward_input[0].astype(jnp.float32) + mixed.astype(jnp.float32)).astype(
        jnp.bfloat16
    )
    ahead_wide, ahead_inv, ahead_normed = normalize(resid_ahead, gain)
    ahead_probs, ahead_selects = routing(ahead_normed, forward_ids[0], table)
    ahead_target = place_slots(ahead_selects, capacity)
    ahead_buffer = pack_rows(ahead_normed, ahead_target, experts, capacity)
    behind_wide, behind_inv, behind_normed = normalize(backward_input[0], gain)
    behind_probs, behind_selects = routing(behind_normed, backward_ids[0], table)
    behind_target = place_slots(behind_selects, capacity)
    rows_buffer = pack_rows(behind_normed, behind_target, experts, capacity)
    grads_buffer = pack_rows(output_grad[0], behind_target, experts, capacity)
    arrived = lax.all_to_all(ahead_buffer, "expert", split_axis=0, concat_axis=0, tiled=True)
    produced = scatter_slots(
        expert_ahead(gather_slots(arrived, per_device), gate_local, up_local, down_local), sources
    )
    returned, behind_rows, behind_grads = (
        lax.all_to_all(produced, "expert", split_axis=0, concat_axis=0, tiled=True),
        lax.all_to_all(rows_buffer, "expert", split_axis=0, concat_axis=0, tiled=True),
        lax.all_to_all(grads_buffer, "expert", split_axis=0, concat_axis=0, tiled=True),
    )
    slot_back, slot_weight = expert_behind(
        gather_slots(behind_rows, per_device),
        gather_slots(behind_grads, per_device),
        gate_local,
        up_local,
        down_local,
    )
    input_back, weight_back = (
        lax.all_to_all(
            scatter_slots(slot_back, sources), "expert", split_axis=0, concat_axis=0, tiled=True
        ),
        lax.all_to_all(
            scatter_slots(slot_weight, sources), "expert", split_axis=0, concat_axis=0, tiled=True
        ),
    )
    ahead_rows = unpack_rows(returned, ahead_target).astype(jnp.float32)
    ahead_output = (ahead_wide + jnp.sum(ahead_probs[:, :, None] * ahead_rows, axis=1)).astype(
        jnp.bfloat16
    )
    input_rows = unpack_rows(input_back, behind_target).astype(jnp.float32)
    weight_rows = weight_back.reshape(-1)[behind_target].astype(jnp.float32)
    normed_grad = jnp.sum(behind_probs[:, :, None] * input_rows, axis=1)
    logit_terms = behind_probs * (
        weight_rows - jnp.sum(behind_probs * weight_rows, axis=-1, keepdims=True)
    )
    logit_grad = jnp.sum(jnp.where(behind_selects, logit_terms[:, :, None], 0.0), axis=1).astype(
        jnp.bfloat16
    )
    normed_grad = normed_grad + jnp.dot(logit_grad, table.T, preferred_element_type=jnp.float32)
    grad_factor = (tokens * sources) ** (-0.5)
    router_term = (
        jnp.dot(behind_normed.T, logit_grad, preferred_element_type=jnp.float32) * grad_factor
    )
    scaled_grad = normed_grad * gain
    resid_grad = behind_inv * (
        scaled_grad
        - behind_wide
        * behind_inv
        * behind_inv
        * jnp.mean(scaled_grad * behind_wide, axis=-1, keepdims=True)
    )
    gain_term = jnp.sum(normed_grad * behind_wide * behind_inv, axis=0) * grad_factor
    input_grad = (output_grad[0].astype(jnp.float32) + resid_grad).astype(jnp.bfloat16)
    router_part, gain_part = (
        lax.psum_scatter(router_term, "expert", scatter_dimension=0, tiled=True),
        lax.psum_scatter(gain_term, "expert", scatter_dimension=0, tiled=True),
    )
    crossing = extended(jnp.stack([input_grad, ahead_output]), (("pipe", 0),), 1)
    return (crossing[0][None], crossing[3][None], router_part[None], gain_part[None])


TILE = 256
SUB = 4
AT_ONCE = 2
VMEM_LIMIT = 60 * 2**20


def fits(operands):
    experts, fan_out = (operands[8].shape[2], operands[12].shape[2])
    tokens, width = operands[0].shape[1:]
    hidden = operands[9].shape[3]
    return (
        lax.axis_size("expert") == 2**3
        and experts == lax.axis_size("expert")
        and experts <= 2 * fan_out
        and lax.axis_size("pipe") > 1
        and tokens == HEAD_DIM
        and operands[4].shape[1] == tokens
        and width % TILE == 0
        and hidden % TILE == 0
    )


def section_kernel(
    length_ref,
    fin_ref,
    q_ref,
    nk_ref,
    nv_ref,
    ck_ref,
    cv_ref,
    gain_ref,
    router_ref,
    gate_ref,
    up_ref,
    down_ref,
    fids_ref,
    bin_ref,
    bids_ref,
    og_ref,
    out_fwd,
    out_back,
    out_sums,
    gat,
    gate_v,
    up_v,
    down_v,
    part,
    sibr,
    rx,
    act_a,
    act_b,
    wacc,
    pcol,
    ptab,
    wgs,
    wgr,
    rgp,
    rgr,
    x_v,
    fin_v,
    q_v,
    k_v,
    v_v,
    resid_v,
    staged,
    table,
    lg_rows,
    gacc,
    local_sem,
    gsend,
    grecv,
    ssend,
    srecv,
    xsend,
    xrecv,
    zsend,
    zrecv,
    tsend,
    trecv,
):
    tokens, width = fin_ref.shape
    hidden_tiles = gate_v.shape[0]
    wide_tiles = width // TILE
    half = tokens // 2
    small = half // SUB
    experts = ptab.shape[2]
    group = ptab.shape[1]
    heads = width // HEAD_DIM
    f32, bf16 = jnp.float32, jnp.bfloat16
    nt = (((1,), (1,)), ((), ()))

    me = lax.axis_index("expert")
    core, at_x, at_y = me % 2, (me // 2) % 2, me // 4
    pipe, pipes = lax.axis_index("pipe"), lax.axis_size("pipe")
    following, previous = (pipe + 1) % pipes, (pipe + pipes - 1) % pipes

    def peer(j):
        a = 1 - core if j % 2 else core
        b = 1 - at_x if (j // 2) % 2 else at_x
        c = 1 - at_y if j // 4 else at_y
        return (c * 2 + b) * 2 + a

    def at(j):
        return {"expert": peer(j)}

    SIB, XN, YN = 1, 2, 4

    def remote(src, dst, send, recv, where):
        return pltpu.make_async_remote_copy(
            src_ref=src,
            dst_ref=dst,
            send_sem=send,
            recv_sem=recv,
            device_id=where,
            device_id_type=pl.DeviceIdType.MESH,
        )

    gather_plan = (
        (0, 0, 0, tokens, tokens, SIB),
        (0, 0, 1, 0, half, XN),
        (0, half, 1, half, half, XN),
        (0, half, 2, half, half, YN),
        (0, 0, 2, 0, half, YN),
        (1, 0, 3, 0, half, YN),
        (2, half, 3, half, half, XN),
        (1, 0, 1, tokens, half, SIB),
        (1, half, 1, tokens + half, half, SIB),
        (2, 0, 2, tokens, half, SIB),
        (2, half, 2, tokens + half, half, SIB),
        (3, 0, 3, tokens, half, SIB),
        (3, half, 3, tokens + half, half, SIB),
    )

    def gcopy(a, i):
        sb, sr, tb, tr, rows, j = gather_plan[i]
        return remote(
            gat.at[a, sb, pl.ds(sr, rows)],
            gat.at[a, tb, pl.ds(tr, rows)],
            gsend.at[a, i],
            grecv.at[a, i],
            at(j),
        )

    def scopy(m, r):
        return remote(
            part.at[m, r, pl.ds(tokens, tokens)],
            sibr.at[m, r],
            ssend.at[m, r],
            srecv.at[m, r],
            at(SIB),
        )

    reduce_plan = ((3, 0, XN), (1, 0, XN), (1, half, XN), (3, half, YN), (2, half, YN), (2, 0, YN))

    def xcopy(m, k, q):
        r, row, j = reduce_plan[k]
        return remote(
            part.at[m, r, pl.ds(row + q * small, small)],
            rx.at[m, k, pl.ds(q * small, small)],
            xsend.at[m, k, q],
            xrecv.at[m, k, q],
            at(j),
        )

    def zcopy(m, i):
        rows = pl.ds(i * small, small)
        out, there = (out_fwd, following) if m else (out_back, previous)
        return remote(
            staged.at[m, rows], out.at[rows], zsend.at[m, i], zrecv.at[m, i], {"pipe": there}
        )

    def tcopy(kind, j):
        src, dst = (
            (ptab.at[0, 0], ptab.at[0, j]),
            (ptab.at[1, 0], ptab.at[1, j]),
            (wgs.at[j], wgr.at[j]),
            (rgp.at[peer(j)], rgr.at[j]),
        )[kind]
        return remote(src, dst, tsend.at[kind, j], trecv.at[kind, j], at(j))

    loads = [
        (og_ref, gat.at[0, 0, pl.ds(0, tokens)]),
        (bin_ref, x_v),
        (q_ref, q_v),
        (ck_ref, k_v.at[pl.ds(0, tokens)]),
        (nk_ref, k_v.at[pl.ds(tokens, tokens)]),
        (cv_ref, v_v.at[pl.ds(0, tokens)]),
        (nv_ref, v_v.at[pl.ds(tokens, tokens)]),
        (fin_ref, fin_v),
    ]
    for t in range(hidden_tiles):
        cols = pl.ds(t * TILE, TILE)
        loads += [
            (gate_ref.at[:, cols], gate_v.at[t]),
            (up_ref.at[:, cols], up_v.at[t]),
            (down_ref.at[cols], down_v.at[t]),
        ]
    loads = [
        pltpu.make_async_copy(src, dst, local_sem.at[i]) for i, (src, dst) in enumerate(loads)
    ]
    for copy in loads:
        copy.start()

    barrier = pltpu.get_barrier_semaphore()
    for j in range(1, group):
        pl.semaphore_signal(barrier, inc=1, device_id=at(j), device_id_type=pl.DeviceIdType.MESH)
    for there in (following, previous):
        pl.semaphore_signal(
            barrier, inc=1, device_id={"pipe": there}, device_id_type=pl.DeviceIdType.MESH
        )
    pl.semaphore_wait(barrier, group - 1 + 2)

    loads[0].wait()
    for i in (1, 3, 2, 4, 0):
        gcopy(0, i).start()

    table[...] = jnp.zeros_like(table)
    rows16 = rgp.shape[1]
    table[0:rows16, :] = jnp.concatenate(
        [router_ref[...].astype(f32), jnp.zeros((rows16 - experts, width), f32)], axis=0
    ).astype(bf16)

    def normalize_rows(source, a):
        def step(i, carry):
            rows = pl.ds(pl.multiple_of(i * 32, 32), 32)
            x = source[rows, :].astype(f32)
            inv = lax.rsqrt(jnp.mean(x * x, axis=-1, keepdims=True) + epsilon)
            gat[a, 0, rows, :] = (x * inv * gain_ref[...]).astype(bf16)
            return carry

        lax.fori_loop(0, tokens // 32, step, 0)

    expert_row = lax.broadcasted_iota(jnp.int32, (experts, tokens), 0)

    def chosen_mask(ids_ref):
        ids = ids_ref[...]
        mask = ids[0:1, :] == expert_row
        for k in range(1, ids.shape[0]):
            mask = mask | (ids[k : k + 1, :] == expert_row)
        return mask

    def route(a, ids_ref, m):
        logits = lax.dot_general(
            table[...], gat[a, 0, 0:tokens, :], nt, preferred_element_type=f32
        )[0:experts, :]
        mask = chosen_mask(ids_ref)
        top = jnp.max(jnp.where(mask, logits, far_below), axis=0, keepdims=True)
        lifted = jnp.where(mask, jnp.exp(jnp.where(mask, logits - top, 0.0)), 0.0)
        ptab[m, 0] = lifted / jnp.sum(lifted, axis=0, keepdims=True)

    loads[1].wait()
    normalize_rows(x_v, 1)
    for i in (1, 3, 2, 4, 0):
        gcopy(1, i).start()
    route(1, bids_ref, 0)
    for j in range(1, group):
        tcopy(0, j).start()

    for i in range(2, 8):
        loads[i].wait()
    length = length_ref[0, 0]

    position = lax.broadcasted_iota(jnp.int32, (tokens, 2 * tokens), 1)
    query_pos = lax.broadcasted_iota(jnp.int32, (tokens, 2 * tokens), 0)
    visible = ((position < tokens) & (position < length)) | (
        (position >= tokens) & (position - tokens <= query_pos)
    )

    def some_heads(i, carry):
        shared = i // (HEADS // KV_HEADS // AT_ONCE)
        kv_cols = pl.ds(pl.multiple_of(shared * HEAD_DIM, HEAD_DIM), HEAD_DIM)
        keys, values = k_v[:, kv_cols], v_v[:, kv_cols]
        results = []
        for u in range(AT_ONCE):
            h = i * AT_ONCE + u
            cols = pl.ds(pl.multiple_of(h * HEAD_DIM, HEAD_DIM), HEAD_DIM)
            scores = lax.dot_general(q_v[:, cols], keys, nt, preferred_element_type=f32)
            scores = jnp.where(visible, scores * HEAD_DIM ** (-0.5), far_below)
            lifted = jnp.exp(scores - jnp.max(scores, axis=-1, keepdims=True))
            weights = (lifted / jnp.sum(lifted, axis=-1, keepdims=True)).astype(bf16)
            mixed = jnp.dot(weights, values, preferred_element_type=f32).astype(bf16)
            results.append(
                (cols, (fin_v[:, cols].astype(f32) + mixed.astype(f32)).astype(bf16))
            )
        for cols, rows in results:
            resid_v[:, cols] = rows
        return carry

    lax.fori_loop(0, heads // AT_ONCE, some_heads, 0)
    normalize_rows(resid_v, 2)
    route(2, fids_ref, 1)
    for j in range(1, group):
        tcopy(1, j).start()
    for copy in loads[8:]:
        copy.wait()
    for kind in (0, 1):
        for j in range(1, group):
            tcopy(kind, j).wait_recv()

    def share_column(m, r):
        for s in range(2):
            row = jnp.sum(jnp.where(expert_row == me, ptab[m, 2 * r + s], 0.0), axis=0, keepdims=True)
            pcol[s * tokens : (s + 1) * tokens, :] = jnp.broadcast_to(row, (tokens, tokens)).T

    def behind_block(r):
        wacc[...] = jnp.zeros_like(wacc)

        def tile(t, carry):
            rows = gat[1, r]
            gate_pre = jnp.dot(rows, gate_v[t], preferred_element_type=f32)
            up_pre = jnp.dot(rows, up_v[t], preferred_element_type=f32)
            down_grad = lax.dot_general(gat[0, r], down_v[t], nt, preferred_element_type=f32)
            sig = jax.nn.sigmoid(gate_pre)
            gate_act = gate_pre * sig
            weighed = (gate_act * up_pre).astype(bf16).astype(f32) * down_grad
            folded = weighed[:, 0:tokens]
            for c in range(1, TILE // tokens):
                folded = folded + weighed[:, c * tokens : (c + 1) * tokens]
            wacc[...] += folded
            slope = sig * (1.0 + gate_pre * (1.0 - sig))
            act_a[t] = (down_grad * up_pre * slope).astype(bf16)
            act_b[t] = (down_grad * gate_act).astype(bf16)
            return carry

        lax.fori_loop(0, hidden_tiles, tile, 0)
        for s in range(2):
            row = jnp.sum(wacc[s * tokens : (s + 1) * tokens, :].T, axis=0, keepdims=True)
            wgs[2 * r + s] = jnp.where(expert_row == me, row, 0.0)
        share_column(0, r)

        def back(n, carry):
            cols = pl.ds(pl.multiple_of(n * TILE, TILE), TILE)
            total = jnp.zeros((2 * tokens, TILE), f32)
            for t in range(hidden_tiles):
                total += lax.dot_general(act_a[t], gate_v[t, cols, :], nt, preferred_element_type=f32)
                total += lax.dot_general(act_b[t], up_v[t, cols, :], nt, preferred_element_type=f32)
            part[0, r, :, cols] = (total * pcol[:, 0:1]).astype(bf16)
            return carry

        lax.fori_loop(0, wide_tiles, back, 0)

    def ahead_block(r):
        def tile(t, carry):
            rows = gat[2, r]
            gate_pre = jnp.dot(rows, gate_v[t], preferred_element_type=f32)
            up_pre = jnp.dot(rows, up_v[t], preferred_element_type=f32)
            act_a[t] = (gate_pre * jax.nn.sigmoid(gate_pre) * up_pre).astype(bf16)
            return carry

        lax.fori_loop(0, hidden_tiles, tile, 0)
        share_column(1, r)

        def out(n, carry):
            cols = pl.ds(pl.multiple_of(n * TILE, TILE), TILE)
            total = jnp.zeros((2 * tokens, TILE), f32)
            for t in range(hidden_tiles):
                total += jnp.dot(act_a[t], down_v[t, :, cols], preferred_element_type=f32)
            part[1, r, :, cols] = (total * pcol[:, 0:1]).astype(bf16)
            return carry

        lax.fori_loop(0, wide_tiles, out, 0)

    def add_rows(m, r, base, count, other, other_base):
        def step(i, carry):
            to = pl.ds(pl.multiple_of(base + i * 16, 16), 16)
            since = pl.ds(pl.multiple_of(other_base + i * 16, 16), 16)
            part[m, r, to, :] = (
                part[m, r, to, :].astype(f32) + other[since, :].astype(f32)
            ).astype(bf16)
            return carry

        lax.fori_loop(0, count // 16, step, 0)

    def join_sibling(m, r):
        scopy(m, r).wait_recv()
        add_rows(m, r, 0, tokens, sibr.at[m, r], 0)

    def send_block(m, r):
        join_sibling(m, r)
        for q in range(SUB):
            for k in ((), (1,), (4,), (0, 3))[r]:
                xcopy(m, k, q).start()

    def second_phase(m):
        for q in range(SUB):
            xcopy(m, 0, q).wait_recv()
            add_rows(m, 2, q * small, small, rx.at[m, 0], q * small)
            xcopy(m, 5, q).start()
            xcopy(m, 3, q).wait_recv()
            add_rows(m, 1, half + q * small, small, rx.at[m, 3], q * small)
            xcopy(m, 2, q).start()

    def forward_first(a):
        gcopy(a, 1).wait_recv()
        gcopy(a, 5).start()
        gcopy(a, 7).start()
        gcopy(a, 3).wait_recv()
        gcopy(a, 6).start()
        gcopy(a, 10).start()

    def forward_second(a):
        gcopy(a, 2).wait_recv()
        gcopy(a, 8).start()
        gcopy(a, 4).wait_recv()
        gcopy(a, 9).start()

    def forward_third(a):
        gcopy(a, 5).wait_recv()
        gcopy(a, 11).start()
        gcopy(a, 6).wait_recv()
        gcopy(a, 12).start()

    def arrived(a, *which):
        for i in which:
            gcopy(a, i).wait_recv()

    def total_rows(m, i):
        rows = pl.ds(i * small, small)
        side, q = i // SUB, i % SUB
        inner = pl.ds(q * small, small)
        near, far = (4, 2) if side else (1, 5)
        xcopy(m, near, q).wait_recv()
        xcopy(m, far, q).wait_recv()
        return rows, near, far, inner

    def finish_behind(i):
        rows, near, far, inner = total_rows(0, i)
        for u in range(small // 16):
            at_rows = pl.ds(i * small + u * 16, 16)
            sub_rows = pl.ds((i % SUB) * small + u * 16, 16)
            normed_grad = (
                part[0, 0, at_rows, :].astype(f32)
                + rx[0, near, sub_rows, :].astype(f32)
                + rx[0, far, sub_rows, :].astype(f32)
                + jnp.dot(lg_rows[at_rows, :], table[...], preferred_element_type=f32)
            )
            x = x_v[at_rows, :].astype(f32)
            inv = lax.rsqrt(jnp.mean(x * x, axis=-1, keepdims=True) + epsilon)
            scaled = normed_grad * gain_ref[...]
            slope = jnp.mean(scaled * x, axis=-1, keepdims=True)
            resid_grad = inv * (scaled - x * (inv * inv * slope))
            gacc[...] += jnp.sum(normed_grad * x * inv, axis=0, keepdims=True)
            staged[0, at_rows, :] = (
                gat[0, 0, at_rows, :].astype(f32) + resid_grad
            ).astype(bf16)
        zcopy(0, i).start()

    def finish_ahead(i):
        rows, near, far, inner = total_rows(1, i)
        total = (
            part[1, 0, rows, :].astype(f32)
            + rx[1, near, inner, :].astype(f32)
            + rx[1, far, inner, :].astype(f32)
        )
        staged[1, rows, :] = (resid_v[rows, :].astype(f32) + total).astype(bf16)
        zcopy(1, i).start()

    order = [side * SUB + q for q in range(SUB) for side in range(2)]

    def finish_all_behind():
        wrows = wgs[0]
        for j in range(1, group):
            tcopy(2, j).wait_recv()
            wrows = wrows + wgr[j]
        probs = ptab[0, 0]
        logit_grad = probs * (wrows - jnp.sum(probs * wrows, axis=0, keepdims=True))
        padded = jnp.concatenate([logit_grad, jnp.zeros((tokens - experts, tokens), f32)], axis=0)
        lg_rows[...] = padded.T.astype(bf16)
        gacc[...] = jnp.zeros_like(gacc)

        for i in order:
            finish_behind(i)
        factor = (tokens * group) ** (-0.5)
        pad_rows = rgp.shape[1]
        lg_short = padded[0:pad_rows, :].astype(bf16)
        span = rgp.shape[2]
        which = lax.broadcasted_iota(jnp.int32, (pad_rows, span), 0)
        for d in range(group):
            cols = slice(d * span, (d + 1) * span)
            grads = jnp.dot(lg_short, gat[1, 0, 0:tokens, cols], preferred_element_type=f32)
            rgp[d] = jnp.where(which == experts, gacc[:, cols], grads) * factor
        for j in range(1, group):
            tcopy(3, j).start()


    forward_first(0)
    forward_second(0)

    def stage(step, carry):
        @pl.when(step == 0)
        def _():
            arrived(0, 0)
            arrived(1, 0)

        @pl.when(step == 1)
        def _():
            forward_first(1)
            forward_second(1)
            for i in (1, 3, 2, 4, 0):
                gcopy(2, i).start()
            arrived(0, 7, 8)
            arrived(1, 7, 8)

        @pl.when(step == 2)
        def _():
            arrived(0, 9, 10)
            arrived(1, 9, 10)
            send_block(0, 0)

        @pl.when(step == 3)
        def _():
            forward_third(0)
            forward_third(1)
            send_block(0, 1)
            send_block(0, 2)
            forward_first(2)
            arrived(0, 11, 12)
            arrived(1, 11, 12)

        @pl.when(step == 4)
        def _():
            for j in range(1, group):
                tcopy(2, j).start()
            send_block(0, 3)
            forward_second(2)
            forward_third(2)
            arrived(2, 11, 12)

        @pl.when(step == 5)
        def _():
            send_block(1, 3)
            arrived(2, 9, 10)

        @pl.when(step == 6)
        def _():
            second_phase(0)
            send_block(1, 2)
            arrived(2, 7, 8)

        @pl.when(step == 7)
        def _():
            send_block(1, 1)
            arrived(2, 0)
            second_phase(1)
            finish_all_behind()

        @pl.when(step < 4)
        def _():
            behind_block(step)

        @pl.when(step >= 4)
        def _():
            ahead_block(7 - step)

        for s in range(8):

            @pl.when(step == s)
            def _(s=s):
                scopy(s // 4, s if s < 4 else 7 - s).start()

        return carry

    lax.fori_loop(0, 8, stage, 0)
    send_block(1, 0)
    for i in order:
        finish_ahead(i)

    sums = rgp[me]
    for j in range(1, group):
        tcopy(3, j).wait_recv()
        sums = sums + rgr[j]
    out_sums[...] = sums

    for a in range(3):
        for i in range(len(gather_plan)):
            gcopy(a, i).wait_send()
    for kind in range(4):
        for j in range(1, group):
            tcopy(kind, j).wait_send()
    for m in range(2):
        for r in range(4):
            scopy(m, r).wait_send()
        for k in range(len(reduce_plan)):
            for q in range(SUB):
                xcopy(m, k, q).wait_send()
        for i in range(2 * SUB):
            zcopy(m, i).wait()


def place_kernel(fwd_ref, back_ref, sums_ref, fwd_out, back_out, router_out, gain_out, sems):
    experts = router_out.shape[0]
    copies = [
        pltpu.make_async_copy(fwd_ref, fwd_out, sems.at[0]),
        pltpu.make_async_copy(back_ref, back_out, sems.at[1]),
    ]
    for copy in copies:
        copy.start()
    router_out[...] = sums_ref[0:experts, :]
    gain_out[...] = sums_ref[experts : experts + 1, :]
    for copy in copies:
        copy.wait()


def kernel_body(
    forward_input,
    queries,
    new_keys,
    new_values,
    cache_keys,
    cache_values,
    context_lengths,
    norm_gain,
    router,
    gate_weight,
    up_weight,
    down_weight,
    forward_ids,
    backward_input,
    backward_ids,
    output_grad,
):
    tokens, width = forward_input.shape[1:]
    experts = router.shape[2]
    group = lax.axis_size("expert")
    hidden = gate_weight.shape[3]
    tiles = hidden // TILE
    pad_experts = experts + 8
    half = tokens // 2
    kv_width = cache_keys.shape[2]
    f32, bf16 = jnp.float32, jnp.bfloat16
    table = router[0].T
    hbm = pl.BlockSpec(memory_space=pl.ANY)
    near = pl.BlockSpec(memory_space=pltpu.VMEM)
    copies = 13
    dma = pltpu.SemaphoreType.DMA
    out_fwd, out_back, sums = pl.pallas_call(
        section_kernel,
        out_shape=(
            jax.ShapeDtypeStruct((tokens, width), bf16),
            jax.ShapeDtypeStruct((tokens, width), bf16),
            jax.ShapeDtypeStruct((pad_experts, width // group), f32),
        ),
        in_specs=[
            pl.BlockSpec(memory_space=pltpu.SMEM),
            hbm,
            hbm,
            hbm,
            hbm,
            hbm,
            hbm,
            near,
            near,
            hbm,
            hbm,
            hbm,
            near,
            hbm,
            near,
            hbm,
        ],
        out_specs=(hbm, hbm, near),
        scratch_shapes=[
            pltpu.VMEM((3, 4, 2 * tokens, width), bf16),
            pltpu.VMEM((tiles, width, TILE), bf16),
            pltpu.VMEM((tiles, width, TILE), bf16),
            pltpu.VMEM((tiles, TILE, width), bf16),
            pltpu.VMEM((2, 4, 2 * tokens, width), bf16),
            pltpu.VMEM((2, 4, tokens, width), bf16),
            pltpu.VMEM((2, 6, half, width), bf16),
            pltpu.VMEM((tiles, 2 * tokens, TILE), bf16),
            pltpu.VMEM((tiles, 2 * tokens, TILE), bf16),
            pltpu.VMEM((2 * tokens, tokens), f32),
            pltpu.VMEM((2 * tokens, tokens), f32),
            pltpu.VMEM((2, group, experts, tokens), f32),
            pltpu.VMEM((group, experts, tokens), f32),
            pltpu.VMEM((group, experts, tokens), f32),
            pltpu.VMEM((group, pad_experts, width // group), f32),
            pltpu.VMEM((group, pad_experts, width // group), f32),
            pltpu.VMEM((tokens, width), bf16),
            pltpu.VMEM((tokens, width), bf16),
            pltpu.VMEM((tokens, width), bf16),
            pltpu.VMEM((2 * tokens, kv_width), bf16),
            pltpu.VMEM((2 * tokens, kv_width), bf16),
            pltpu.VMEM((tokens, width), bf16),
            pltpu.VMEM((2, tokens, width), bf16),
            pltpu.VMEM((tokens, width), bf16),
            pltpu.VMEM((tokens, tokens), bf16),
            pltpu.VMEM((1, width), f32),
            dma((8 + 3 * tiles,)),
            dma((3, copies)),
            dma((3, copies)),
            dma((2, 4)),
            dma((2, 4)),
            dma((2, 6, SUB)),
            dma((2, 6, SUB)),
            dma((2, 2 * SUB)),
            dma((2, 2 * SUB)),
            dma((4, group)),
            dma((4, group)),
        ],
        compiler_params=pltpu.CompilerParams(
            collective_id=0, has_side_effects=True, vmem_limit_bytes=VMEM_LIMIT
        ),
    )(
        context_lengths,
        forward_input[0],
        queries[0],
        new_keys[0],
        new_values[0],
        cache_keys[0],
        cache_values[0],
        norm_gain,
        table,
        gate_weight[0, 0],
        up_weight[0, 0],
        down_weight[0, 0],
        forward_ids[0].T,
        backward_input[0],
        backward_ids[0].T,
        output_grad[0],
    )
    span = width // group
    out_fwd, out_back, router_part, gain_part = pl.pallas_call(
        place_kernel,
        out_shape=(
            jax.ShapeDtypeStruct((tokens, width), bf16),
            jax.ShapeDtypeStruct((tokens, width), bf16),
            jax.ShapeDtypeStruct((experts, span), f32),
            jax.ShapeDtypeStruct((1, span), f32),
        ),
        in_specs=[hbm, hbm, near],
        out_specs=(hbm, hbm, near, near),
        scratch_shapes=[dma((2,))],
    )(out_fwd, out_back, sums)
    return (out_fwd[None], out_back[None], router_part.T[None], gain_part)


def body(*operands):
    return (kernel_body if fits(operands) else routed_body)(*operands)


def solution(mesh):
    placed = (
        P("pipe", "expert", None),
        P("pipe", "expert", None),
        P("pipe", "expert", None),
        P("pipe", "expert", None),
        P("pipe", "expert", None),
        P("pipe", "expert", None),
        P("pipe", "expert"),
        P("pipe", None),
        P("pipe", None, None),
        P("pipe", "expert", None, None),
        P("pipe", "expert", None, None),
        P("pipe", "expert", None, None),
        P("pipe", "expert", None),
        P("pipe", "expert", None),
        P("pipe", "expert", None),
        P("pipe", "expert", None),
    )
    return jax.shard_map(
        body,
        mesh=mesh,
        in_specs=placed,
        out_specs=(
            P("pipe", "expert", None),
            P("pipe", "expert", None),
            P("pipe", "expert", None),
            P("pipe", "expert"),
        ),
        check_vma=False,
    )
```
